32 devices in a mesh: expert: 8 (over z, y), hidden: 4 (over x, core).
Axes of the slice: x: 2, y: 2, z: 4, core: 2. Of those that a mesh axis runs over, the one named last changes fastest.
Arguments:
- inputs: bfloat16 [8192, 1024], P(('expert', 'hidden')), may hold values from -6 to 6
- first_gain: float32 [1024], replicated, may hold values from 0.1 to 1.9
- query_weight: bfloat16 [1024, 1024], replicated, may hold values from -0.25 to 0.25
- key_weight: bfloat16 [1024, 512], replicated, may hold values from -0.25 to 0.25
- value_weight: bfloat16 [1024, 512], replicated, may hold values from -0.1875 to 0.1875
- out_weight: bfloat16 [1024, 1024], replicated, may hold values from -0.75 to 0.75
- second_gain: float32 [1024], replicated, may hold values from 0.1 to 1.9
- router_weight: bfloat16 [1024, 32], replicated, may hold values from -0.09375 to 0.09375
- gate_weight: bfloat16 [32, 512, 1024], P('expert', 'hidden'), may hold values from -0.1875 to 0.1875
- up_weight: bfloat16 [32, 512, 1024], P('expert', 'hidden'), may hold values from -0.1875 to 0.1875
- down_weight: bfloat16 [32, 512, 1024], P('expert', 'hidden'), may hold values from -1 to 1
- routes: int32 [8192, 8], P(('expert', 'hidden')), may hold values from 0 to 31, all different within a row
- segments: int32 [8192], P(('expert', 'hidden')), may hold values from 0 to 3, as said below
- cotangent: bfloat16 [8192, 1024], P(('expert', 'hidden')), may hold values from -6 to 6
Outputs:
- block_out: bfloat16 [8192, 1024], P(('expert', 'hidden'))
- input_grad: bfloat16 [8192, 1024], P(('expert', 'hidden'))
- first_gain_grad: float32 [1024], P(('expert', 'hidden'))
- query_grad: float32 [1024, 1024], P(('expert', 'hidden'))
- key_grad: float32 [1024, 512], P(('expert', 'hidden'))
- value_grad: float32 [1024, 512], P(('expert', 'hidden'))
- out_weight_grad: float32 [1024, 1024], P(('expert', 'hidden'))
- second_gain_grad: float32 [1024], P(('expert', 'hidden'))
- router_grad: float32 [1024, 32], P(('expert', 'hidden'))
- gate_grad: float32 [32, 512, 1024], P('expert', 'hidden')
- up_grad: float32 [32, 512, 1024], P('expert', 'hidden')
- down_grad: float32 [32, 512, 1024], P('expert', 'hidden')
The draws below stay inside these ranges and needn't reach their ends.
Inputs may be any that keep to these rules, and one draw needn't show every extreme that they name: `routes`: each row names 8 different experts. `segments`: along each sequence of 1024 tokens the ids start at 0, never fall, and end at 3.
All inputs are finite; a program needn't handle non-finite values.
Results may differ from the reference program's by a relative error of at most 0.018.
Values may be sent and summed in bfloat16 or wider, within the bound.
No kernel may reach another device: no remote copies, remote signals or barrier semaphores. Data moves between devices by JAX's collectives and lax.ppermute only.
A program may use at most 192 MiB of HBM per device.

```python
import jax
import jax.numpy as jnp
from jax import lax

D = 1024
HEADS = 16
KV_HEADS = 8
HEAD_DIM = 64
FF = 512
EXPERTS = 32
TOP = 8
TOK_DEV = 256
CAP = 128
SEQ_LEN = 1024
SEQS = 8
TOKENS = 8192


def draw_segments(key, part):
    key = jax.random.fold_in(key, 7)
    first_key, last_key = jax.random.split(key, 2)
    starts = jax.random.randint(first_key, (SEQS, 1), 2, TOK_DEV // 2 + 2)
    finish = SEQ_LEN - 1 - jax.random.randint(last_key, (SEQS, 1), 0, TOK_DEV // 2)
    index = jnp.arange(SEQ_LEN, dtype=jnp.int32)[None, :]
    flags = (index == 1) | (index == starts) | (index == finish)
    document = jnp.cumsum(flags.astype(jnp.int32), axis=1)
    return document.reshape(-1).astype(jnp.int32)


def with_spikes(values, stream_key, source, target, shards_of, factor):
    def block_of(dim):
        return (jnp.arange(values.shape[dim]) // (values.shape[dim] // shards_of)).reshape((-1,) + (1,) * (values.ndim - 1 - dim))

    near = jax.random.permutation(stream_key, shards_of)[block_of(target)]
    other_side = (block_of(target) + shards_of // 2) % shards_of
    return jnp.where((block_of(source) == near) | (block_of(source) == other_side), factor * values, values)


def steps_of(own_key, extent, cuts, least, largest):
    gain = 1.0
    for dim, blocks in cuts:
        heights = jax.random.uniform(jax.random.fold_in(jax.random.fold_in(own_key, 6), dim), (blocks,), jnp.float32, least / len(cuts), largest / len(cuts))
        gain = gain * jnp.repeat(jnp.exp(heights), extent[dim] // blocks).reshape((-1,) + (1,) * (len(extent) - 1 - dim))
    return gain


def picks_of(key, rows, count, top, lift):
    ranking = jax.random.permutation(jax.random.fold_in(key, 1), count)
    boost = ranking
    for power in range(3):
        boost = boost * boost // count
    boost = boost * lift // count
    chance = jax.random.randint(jax.random.fold_in(key, 2), (rows, count), 0, 4096) + boost
    sure = jax.random.permutation(jax.random.fold_in(key, 3), rows)[jnp.arange(count) % rows]
    chance = jnp.where(jnp.arange(rows)[:, None] == sure[None, :], 1 << 14, chance)
    score = chance * count + jnp.arange(count)
    return lax.top_k(score.astype(jnp.int32), top)[1].astype(jnp.int32)


def normal_values(stream_key, extent, deviation, most, shards=(), held_as=jnp.bfloat16):
    drawn = deviation * jax.random.normal(stream_key, extent, jnp.float32)
    if shards:
        drawn = drawn * steps_of(stream_key, extent, shards, -0.22, 0.18)
    return jnp.clip(drawn, -most, most).astype(held_as)


def heavy_noise(stream_key, shape, width, limit, shards, heavy, held_as=jnp.bfloat16):
    array = width * jax.random.normal(stream_key, shape, jnp.float32)
    if shards:
        array = array * steps_of(stream_key, shape, shards, -0.22, 0.18)
    return jnp.clip(with_spikes(array, jax.random.fold_in(stream_key, 3), *heavy), -limit, limit).astype(held_as)


def setup_inputs(seed: int = 0) -> dict:
    splits = jax.random.split(jax.random.key(seed), 15)
    inputs = heavy_noise(splits[0], (TOKENS, D), 1.0, 6.0, ((0, 32),), (0, 1, 32, 2.75))
    first_gain = jnp.clip(1.0 + 0.18 * jax.random.normal(splits[1], (D,), jnp.float32), 0.1, 1.9)
    query_weight = normal_values(splits[2], (D, HEADS * HEAD_DIM), (D // 2) ** -0.5, 0.25)
    key_weight = normal_values(splits[3], (D, KV_HEADS * HEAD_DIM), (D // 2) ** -0.5, 0.25)
    value_weight = normal_values(splits[4], (D, KV_HEADS * HEAD_DIM), D ** -0.5, 0.1875)
    out_weight = normal_values(splits[5], (HEADS * HEAD_DIM, D), (D // 16) ** -0.5, 0.75)
    second_gain = jnp.clip(1.0 + 0.18 * jax.random.normal(splits[6], (D,), jnp.float32), 0.1, 1.9)
    router_weight = normal_values(splits[7], (D, EXPERTS), (4 * D) ** -0.5, 0.09375)
    gate_weight = normal_values(splits[8], (EXPERTS, FF, D), D ** -0.5, 0.1875, ((0, 8), (1, 4)))
    up_weight = normal_values(splits[9], (EXPERTS, FF, D), D ** -0.5, 0.1875, ((0, 8), (1, 4)))
    down_weight = normal_values(splits[10], (EXPERTS, FF, D), (FF // 16) ** -0.5, 1.0, ((0, 8), (1, 4)))
    routes = picks_of(splits[11], TOKENS, EXPERTS, TOP, 2048)
    segments = draw_segments(jax.random.fold_in(splits[14], 71), 0)
    cotangent = normal_values(splits[13], (TOKENS, D), 1.0, 6.0, ((0, 32),))
    return {"inputs": inputs, "first_gain": first_gain, "query_weight": query_weight, "key_weight": key_weight, "value_weight": value_weight, "out_weight": out_weight, "second_gain": second_gain, "router_weight": router_weight, "gate_weight": gate_weight, "up_weight": up_weight, "down_weight": down_weight, "routes": routes, "segments": segments, "cotangent": cotangent}


epsilon = 1e-06
rope_base = 10000.0
masked_score = -1e+30
maximum_precision = lax.Precision.HIGHEST

@jax.custom_vjp
def low(v):
    return lax.optimization_barrier(v.astype(jnp.bfloat16)).astype(jnp.float32)

@jax.custom_vjp
def lowered_backward(v):
    return v

def low_keep(v):
    return (low(v), None)

def low_pass(kept, grad):
    return (grad,)

def back_keep(v):
    return (v, None)

def back_low(kept, grad):
    return (low(grad),)
low.defvjp(low_keep, low_pass)
lowered_backward.defvjp(back_keep, back_low)

def matmul(operand, other_operand):
    return jnp.dot(operand, other_operand, precision=maximum_precision)

def rms_norm(values, gain_vector):
    factor = lax.rsqrt(lax.optimization_barrier(jnp.mean(values * values, axis=-1, keepdims=True)) + epsilon)
    return values * factor * gain_vector

def rotary(values, angles_at, head_size):
    half_size = head_size // 2
    spectrum = rope_base ** (-jnp.arange(half_size, dtype=jnp.float32) * 2.0 / head_size)
    angles = angles_at[:, None] * spectrum[None, :]
    cosine = jnp.cos(angles)[:, None, :]
    sine_of = jnp.sin(angles)[:, None, :]
    front = values[..., :half_size]
    back_half = values[..., half_size:]
    return jnp.concatenate([front * cosine - back_half * sine_of, back_half * cosine + front * sine_of], axis=-1)

def attend(query_head_rows, key_head_rows, value_head_rows, segment_row):
    length = key_head_rows.shape[0]
    attention_scale = HEAD_DIM ** (-0.5)
    attention_scores = lowered_backward(jnp.einsum('nbkc,qbc->bknq', query_head_rows, key_head_rows, precision=maximum_precision) * attention_scale)
    places = jnp.arange(length, dtype=jnp.int32)
    allowed = (segment_row[:, None] == segment_row[None, :]) & (places[None, :] <= places[:, None])
    attention_scores = jnp.where(allowed, attention_scores, masked_score)
    row_peak = lax.optimization_barrier(jnp.max(attention_scores, axis=-1, keepdims=True))
    weights = jnp.exp(attention_scores - row_peak)
    attention_probabilities = low(weights / lax.optimization_barrier(jnp.sum(weights, axis=-1, keepdims=True)))
    return jnp.einsum('ozvn,nob->vozb', attention_probabilities, value_head_rows, precision=maximum_precision)

def dispatch_table(routes):
    blocks = TOKENS // TOK_DEV
    picked = (routes[:, :, None] == jnp.arange(EXPERTS, dtype=jnp.int32)[None, None, :]).astype(jnp.int32)
    expert_loads = lax.optimization_barrier(jnp.sum(picked, axis=1)).reshape(blocks, TOK_DEV, EXPERTS)
    earlier = (jnp.cumsum(expert_loads, axis=1) - expert_loads).reshape(TOKENS, EXPERTS)
    slot_ids = jnp.take_along_axis(earlier, routes, axis=1)
    block_of = (jnp.arange(TOKENS, dtype=jnp.int32) // TOK_DEV)[:, None]
    slot_place = jnp.where(slot_ids < CAP, block_of * CAP + slot_ids, blocks * CAP).astype(jnp.int32)
    pair_ids = jnp.arange(TOKENS * TOP, dtype=jnp.int32).reshape(TOKENS, TOP)
    slot_table = jnp.full((EXPERTS, blocks * CAP), -1, jnp.int32)
    return slot_table.at[routes, slot_place].set(pair_ids, mode='drop')

def reference(inputs, first_gain, query_weight, key_weight, value_weight, out_weight, second_gain, router_weight, gate_weight, up_weight, down_weight, routes, segments, cotangent):
    slot_table = dispatch_table(routes)
    pair_index = jnp.maximum(slot_table, 0).astype(jnp.int32)
    slot_valid = (slot_table >= 0).astype(jnp.float32)
    token_of_pair = (pair_index // TOP).astype(jnp.int32)
    segment_rows = segments.reshape(SEQS, SEQ_LEN)
    group_size = HEADS // KV_HEADS
    places = jnp.tile(jnp.arange(SEQ_LEN, dtype=jnp.float32), SEQS)

    def forward(source, gain_one, query_mat, key_mat, value_mat, out_mat, gain_two, router_mat, gate_mats, up_mats, down_mats):
        normed = low(rms_norm(source, gain_one))
        query_lin = lowered_backward(matmul(normed, query_mat))
        key_lin = lowered_backward(matmul(normed, key_mat))
        value_lin = lowered_backward(matmul(normed, value_mat))
        queries = low(rotary(query_lin.reshape(TOKENS, HEADS, HEAD_DIM), places, HEAD_DIM))
        key_head_rows = low(rotary(key_lin.reshape(TOKENS, KV_HEADS, HEAD_DIM), places, HEAD_DIM))
        values = low(value_lin)

        def one_sequence(carried, pieces):
            local_queries, local_keys, local_values, local_segments = pieces
            mixed_heads = attend(local_queries, local_keys, local_values, local_segments)
            return (carried, mixed_heads.reshape(SEQ_LEN, HEADS * HEAD_DIM))
        unused, mixed_heads = lax.scan(jax.checkpoint(one_sequence), jnp.zeros((), jnp.float32), (queries.reshape(SEQS, SEQ_LEN, KV_HEADS, group_size, HEAD_DIM), key_head_rows.reshape(SEQS, SEQ_LEN, KV_HEADS, HEAD_DIM), values.reshape(SEQS, SEQ_LEN, KV_HEADS, HEAD_DIM), segment_rows))
        attended = low(lowered_backward(mixed_heads.reshape(TOKENS, HEADS * HEAD_DIM)))
        hidden = source + lowered_backward(matmul(attended, out_mat))
        ffn_normed = low(rms_norm(hidden, gain_two))
        logits = lowered_backward(matmul(ffn_normed, router_mat))
        gate_probs = jax.nn.softmax(jnp.take_along_axis(logits, routes, axis=1), axis=-1)
        gate_list = gate_probs.reshape(-1)

        def one_expert(pieces):
            pair_ids, slot_mask, gate_mat, up_mat, down_mat = pieces
            owners = (pair_ids // TOP).astype(jnp.int32)
            expert_rows = lowered_backward(jnp.take(ffn_normed, owners, axis=0) * slot_mask[:, None])
            gate_value = lowered_backward(matmul(expert_rows, gate_mat.T))
            up_value = lowered_backward(matmul(expert_rows, up_mat.T))
            active = low(jax.nn.silu(gate_value) * up_value)
            result = low(lowered_backward(matmul(active, down_mat)))
            return result * (jnp.take(gate_list, pair_ids) * slot_mask)[:, None]
        weighted = lax.map(jax.checkpoint(one_expert), (pair_index, slot_valid, gate_mats, up_mats, down_mats))
        moe_sum = jnp.zeros_like(hidden).at[token_of_pair.reshape(-1)].add(weighted.reshape(-1, D))
        return hidden + moe_sum
    primal = (inputs.astype(jnp.float32), first_gain.astype(jnp.float32), query_weight.astype(jnp.float32), key_weight.astype(jnp.float32), value_weight.astype(jnp.float32), out_weight.astype(jnp.float32), second_gain.astype(jnp.float32), router_weight.astype(jnp.float32), gate_weight.astype(jnp.float32), up_weight.astype(jnp.float32), down_weight.astype(jnp.float32))
    output, pullback = jax.vjp(forward, *primal)
    gradients = pullback(cotangent.astype(jnp.float32))
    return (output.astype(jnp.bfloat16), gradients[0].astype(jnp.bfloat16), gradients[1], gradients[2], gradients[3], gradients[4], gradients[5], gradients[6], gradients[7], gradients[8], gradients[9], gradients[10])
```

```python
import functools

import jax
import jax.numpy as jnp
from jax import lax
from jax.experimental import pallas as pl
from jax.experimental.pallas import tpu as pltpu
from jax.sharding import PartitionSpec as P

HEADS = 16
KV_HEADS = 8
HEAD_DIM = 64
EXPERTS = 32
CAP = 128
KV = KV_HEADS * HEAD_DIM
SIDE = 128
TILE = 256
CHUNK = 8

epsilon = 1e-06
rope_base = 10000.0
masked_score = -1e30
bf16 = jnp.bfloat16
f32 = jnp.float32
ANY = pl.BlockSpec(memory_space=pl.ANY)
SMEM = pl.BlockSpec(memory_space=pltpu.SMEM)
VMEM = pl.BlockSpec(memory_space=pltpu.VMEM)
MIB = 1024 * 1024


def dot(a, b, ca, cb):
    return lax.dot_general(a, b, (((ca,), (cb,)), ((), ())), preferred_element_type=f32)


def rms(values):
    return lax.rsqrt(jnp.mean(values * values, axis=-1, keepdims=True) + epsilon)


def norm_back(grad, values, gain):
    q = rms(values)
    w = grad * gain
    back = q * w - values * (q * q * q) * jnp.mean(w * values, axis=-1, keepdims=True)
    return back, grad * values * q


def turn(u, cosine, sine):
    lane = lax.broadcasted_iota(jnp.int32, u.shape, 1)
    half = HEAD_DIM // 2
    partner = jnp.where(
        lane % HEAD_DIM < half, pltpu.roll(u, 2 * HEAD_DIM - half, 1), pltpu.roll(u, half, 1)
    )
    return u * cosine + partner * sine


def struct(shape, dtype=bf16):
    return jax.ShapeDtypeStruct(shape, dtype)


def call(body, outs, ins, scratch=(), smem=0, name=None, mib=40, flops=10**6, nbytes=10**4):
    return pl.pallas_call(
        body,
        out_shape=outs,
        in_specs=[SMEM] * smem + [VMEM] * (len(ins) - smem),
        out_specs=jax.tree.map(lambda _: VMEM, outs),
        scratch_shapes=list(scratch),
        compiler_params=pltpu.CompilerParams(vmem_limit_bytes=mib * MIB),
        cost_estimate=pl.CostEstimate(flops=flops, bytes_accessed=nbytes, transcendentals=0),
        name=name,
    )(*ins)


def route_body(routes, cot, out):
    tokens, width = cot.shape
    lane = lax.broadcasted_iota(jnp.int32, (tokens, 128), 1)
    named = jnp.zeros((tokens, 128), f32)
    for i in range(routes.shape[1]):
        named = named + jnp.where(lane == routes[:, i : i + 1], 1.0, 0.0)
    row = lax.broadcasted_iota(jnp.int32, (tokens, tokens), 0)
    col = lax.broadcasted_iota(jnp.int32, (tokens, tokens), 1)
    earlier = dot(jnp.where(row > col, 1.0, 0.0).astype(bf16), named.astype(bf16), 1, 0)
    code = jnp.where(named > 0.0, jnp.where(earlier < CAP, earlier, -1.0), -2.0)
    out[:tokens, :] = cot[...]
    out[tokens:, :tokens] = code.T[:EXPERTS].astype(bf16)
    out[tokens:, tokens:] = jnp.zeros((EXPERTS, width - tokens), bf16)


def project_kv_body(place, x, gain, wk, wv, spectrum, seg, kv_out, n_out, c_out, s_out):
    tokens = x.shape[0]
    source = x[...].astype(f32)
    normed = (source * rms(source) * gain[...]).astype(bf16)
    n_out[...] = normed
    at = lax.broadcasted_iota(jnp.int32, (tokens, 128), 0) + place[0]
    lane = lax.broadcasted_iota(jnp.int32, (tokens, 128), 1)
    angles = at.astype(f32) * spectrum[...]
    c = jnp.cos(angles)
    s = jnp.sin(angles)
    s = jnp.where(lane % HEAD_DIM < HEAD_DIM // 2, -s, s)
    c_out[...] = c
    s_out[...] = s
    k = dot(normed, wk[...], 1, 0)
    for i in range(0, KV, 128):
        kv_out[:, i : i + 128] = turn(k[:, i : i + 128], c, s).astype(bf16)
    kv_out[:, KV : 2 * KV] = dot(normed, wv[...], 1, 0).astype(bf16)
    kv_out[:, 2 * KV :] = jnp.broadcast_to(seg[...].astype(f32), (SIDE, tokens)).T.astype(bf16)


def project_q_body(normed, wq, c, s, q_out):
    q = dot(normed[...], wq[...], 1, 0)
    for i in range(0, q.shape[1], 128):
        turned = turn(q[:, i : i + 128], c[...], s[...]).astype(bf16)
        q_out[:, i : i + 128] = turned * bf16(HEAD_DIM**-0.5)


def fill_bias(places, kvs, bias):
    tokens = kvs[0].shape[0]
    mine = kvs[0][:, 2 * KV :].astype(f32)[:, :1]
    row = lax.broadcasted_iota(jnp.int32, (tokens, tokens), 0) + places[0]
    col = lax.broadcasted_iota(jnp.int32, (tokens, tokens), 1)
    for b, kv in enumerate(kvs):
        theirs = kv[:, 2 * KV :].astype(f32).T[:1, :]
        keep = (mine == theirs) & (col + places[b] <= row)
        bias[b] = jnp.where(keep, 0.0, masked_score)


def pair_rows(values, j):
    return jnp.concatenate(
        [values[:, 128 * j : 128 * j + HEAD_DIM], values[:, 128 * j + HEAD_DIM : 128 * j + 128]], 0
    )


def pair_columns(values, tokens):
    return jnp.concatenate([values[:tokens], values[tokens:]], 1)


def scores_of(q2, kv, bias, j):
    tokens = kv.shape[0]
    s = dot(q2, kv[:, HEAD_DIM * j : HEAD_DIM * (j + 1)], 1, 1)
    return (s.reshape(2, tokens, tokens) + bias[None]).reshape(2 * tokens, tokens)


def attend_body(
    nb, places, x, q, *refs
):
    kvs, (wo, gain, router, routes, hid_out, ffn_out, att_out, lse_out, gates_out, bias) = (
        refs[:nb],
        refs[nb:],
    )
    tokens = x.shape[0]
    fill_bias(places, kvs, bias)
    lane = lax.broadcasted_iota(jnp.int32, (tokens, 128), 1)
    lse = jnp.zeros((tokens, 128), f32)
    for j in range(KV_HEADS):
        q2 = pair_rows(q, j)
        s = [scores_of(q2, kv, bias[b], j) for b, kv in enumerate(kvs)]
        peak = functools.reduce(
            jnp.maximum, [jnp.max(t, axis=1, keepdims=True) for t in s]
        )
        p = [jnp.exp(t - peak) for t in s]
        total = sum(jnp.sum(t, axis=1, keepdims=True) for t in p)
        o = sum(
            dot(t.astype(bf16), kv[:, KV + HEAD_DIM * j : KV + HEAD_DIM * (j + 1)], 1, 0)
            for t, kv in zip(p, kvs)
        )
        att_out[:, 128 * j : 128 * j + 128] = pair_columns(o / total, tokens).astype(bf16)
        log_total = peak + jnp.log(total)
        lse = jnp.where(lane == 2 * j, log_total[:tokens], lse)
        lse = jnp.where(lane == 2 * j + 1, log_total[tokens:], lse)
    lse_out[...] = lse
    hidden = x[...].astype(f32) + dot(att_out[...], wo[...], 1, 0)
    hid_out[...] = hidden
    ffn = (hidden * rms(hidden) * gain[...]).astype(bf16)
    ffn_out[...] = ffn
    lane = lax.broadcasted_iota(jnp.int32, (tokens, SIDE), 1)
    named = jnp.zeros((tokens, SIDE), f32)
    for i in range(routes.shape[1]):
        named = named + jnp.where(lane == routes[:, i : i + 1], 1.0, 0.0)
    gates_out[...] = gates_of(dot(ffn, router[...], 1, 0), named, 1)


def gates_of(logits, named, axis):
    logits = jnp.where(named > 0.0, logits, masked_score)
    peak = jnp.max(logits, axis=axis, keepdims=True)
    raised = jnp.where(named > 0.0, jnp.exp(logits - peak), 0.0)
    return raised / jnp.sum(raised, axis=axis, keepdims=True)


def hidden_back_body(
    n, *refs
):
    row_sum = sum(r[...].astype(f32) for r in refs[:n])
    (hid, gates, cot, gain, router, wo, hgrad_out, branch_out, lg_out, gp_out, do_out) = refs[n:]
    width = hid.shape[1]
    side = row_sum[:, width:]
    lane = lax.broadcasted_iota(jnp.int32, side.shape, 1)
    slopes = jnp.where(lane < EXPERTS, side + pltpu.roll(side, SIDE - EXPERTS, 1), 0.0)
    g = gates[...]
    logit_grad = (g * (slopes - jnp.sum(g * slopes, axis=1, keepdims=True))).astype(bf16)
    lg_out[...] = logit_grad
    ffn_grad = row_sum[:, :width] + dot(logit_grad, router[...], 1, 1)
    back, share = norm_back(ffn_grad, hid[...], gain[...])
    gp_out[...] = share.astype(bf16)
    hidden_grad = cot[...].astype(f32) + back
    hgrad_out[...] = hidden_grad
    branch = hidden_grad.astype(bf16)
    branch_out[...] = branch
    do_out[...] = dot(branch, wo[...], 1, 1).astype(bf16)


def attention_back_body(nb, places, do_s, q, *refs):
    kvs = refs[:nb]
    (lse, cosine, sine, dq_out) = refs[nb : nb + 4]
    dkv = refs[nb + 4 : 2 * nb + 4]
    bias = refs[2 * nb + 4]
    tokens = q.shape[0]
    fill_bias(places, kvs, bias)
    c, s = cosine[...], sine[...]
    for j in range(KV_HEADS):
        q2 = pair_rows(q, j)
        do2 = pair_rows(do_s, j)
        lse2 = jnp.concatenate([lse[:, 2 * j : 2 * j + 1], lse[:, 2 * j + 1 : 2 * j + 2]], 0)
        p, dp = [], []
        inner = jnp.zeros((2 * tokens, 1), f32)
        for b, kv in enumerate(kvs):
            pb = jnp.exp(scores_of(q2, kv, bias[b], j) - lse2)
            db = dot(do2, kv[:, KV + HEAD_DIM * j : KV + HEAD_DIM * (j + 1)], 1, 1)
            inner = inner + jnp.sum(pb * db, axis=1, keepdims=True)
            p.append(pb)
            dp.append(db)
        dq2 = jnp.zeros((2 * tokens, HEAD_DIM), f32)
        for b, kv in enumerate(kvs):
            ds = (p[b] * (dp[b] - inner)).astype(bf16)
            dq2 = dq2 + dot(ds, kv[:, HEAD_DIM * j : HEAD_DIM * (j + 1)], 1, 0)
            dkv[b][:, HEAD_DIM * j : HEAD_DIM * (j + 1)] = dot(ds, q2, 0, 0).astype(bf16)
            dkv[b][:, KV + HEAD_DIM * j : KV + HEAD_DIM * (j + 1)] = dot(
                p[b].astype(bf16), do2, 0, 0
            ).astype(bf16)
        dq = pair_columns(dq2, tokens) * HEAD_DIM**-0.5
        dq_out[:, 128 * j : 128 * j + 128] = turn(dq, c, -s).astype(bf16)


def finish_body(
    ka, kb, dq, wq, wk, wv, hgrad, x, gain, cosine, sine, in_out, dkv_out, gp_out
):
    total = ka[...].astype(f32) + kb[...].astype(f32)
    c, s = cosine[...], sine[...]
    for at in range(0, KV, 128):
        dkv_out[:, at : at + 128] = turn(total[:, at : at + 128], c, -s).astype(bf16)
    dkv_out[:, KV:] = total[:, KV:].astype(bf16)
    grad = dot(dq[...], wq[...], 1, 1)
    grad = grad + dot(dkv_out[:, :KV], wk[...], 1, 1) + dot(dkv_out[:, KV:], wv[...], 1, 1)
    back, share = norm_back(grad, x[...].astype(f32), gain[...])
    gp_out[...] = share.astype(bf16)
    in_out[...] = (hgrad[...] + back).astype(bf16)


def weight_body(groups, parts, n_side, me, left, right, *refs):
    sides, (near, far, held) = refs[: 2 * n_side], refs[2 * n_side :]
    width = right.shape[1]

    def put(values, lo, hi):
        v = values.reshape(groups, parts, -1, hi - lo)
        for h in range(parts):
            held[h, :, :, lo:hi] = v[:, h].astype(bf16)

    for at in range(0, width, 512):
        put(dot(left[...], right[:, at : at + 512], 0, 0), at, at + 512)
    if n_side:
        put(
            sum(dot(sides[2 * i][...], sides[2 * i + 1][...], 0, 0) for i in range(n_side)),
            width,
            width + SIDE,
        )
    for m in range(parts):
        (far if m % 2 else near)[m // 2] = held[me[0] ^ m]


def expert_body(blocks, tokens, base, *refs):
    xs, cs = refs[:blocks], refs[blocks : 2 * blocks]
    router, wg_ref, wu_ref, wd_ref = refs[2 * blocks : 2 * blocks + 4]
    refs = refs[2 * blocks + 4 :]
    rows_out = refs[:blocks]
    acts_out, x_out, pg_out, so_out, slots_out, offs_out = refs[blocks : blocks + 6]
    (x_s, c_s, g_t, s_t, xg, cg, so, acts, gs, rg, stage, ob, offs, last, sems, tile_sems) = refs[
        blocks + 6 :
    ]
    e = pl.program_id(0)
    count = pl.num_programs(0)
    width = x_s.shape[2]
    hid = acts.shape[1] // 3
    slot_iota = lax.broadcasted_iota(jnp.int32, (CAP, tokens), 0).astype(f32)
    expert = base[0] + e

    def loads(b):
        return (
            pltpu.make_async_copy(xs[b], x_s.at[b], sems.at[b]),
            pltpu.make_async_copy(cs[b], c_s.at[b], sems.at[blocks + b]),
        )

    def tile_copies(i, at):
        rows = pl.ds(pl.multiple_of(i * TILE, TILE), TILE)
        pairs = ((acts, acts_out), (xg, x_out), (cg, pg_out), (so, so_out))
        return [
            pltpu.make_async_copy(a.at[rows, :], o.at[at, rows, :], tile_sems.at[n, i])
            for n, (a, o) in enumerate(pairs)
        ]

    def wait_tiles(at):
        def wait_one(i, carry):
            for copy in tile_copies(i, at):
                copy.wait()
            return carry

        lax.fori_loop(0, last[0], wait_one, 0)

    @pl.when(e == 0)
    def _():
        for b in range(blocks):
            for load in loads(b):
                load.start()

    @pl.when(e > 0)
    def _():
        wait_tiles(e - 1)

    off = jnp.int32(0)
    for b in range(blocks):

        @pl.when(e == 0)
        def _(b=b):
            for load in loads(b):
                load.wait()
            code = c_s[b, tokens:, :tokens].astype(f32)
            s_t[b] = code
            g_t[b] = gates_of(
                dot(router[...], x_s[b], 1, 1), jnp.where(code > -1.5, 1.0, 0.0), 0
            )

        off = pl.multiple_of(off, 16)
        rows = pl.ds(off, CAP)
        mine = pl.ds(expert, 1)
        slots, gates = s_t[b, mine, :], g_t[b, mine, :]
        slots_out[0, b] = slots
        hit = slot_iota == slots
        pick = jnp.where(hit, 1.0, 0.0).astype(bf16)
        xg[rows, :] = dot(pick, x_s[b], 1, 0).astype(bf16)
        cg[rows, :] = dot(pick, c_s[b, :tokens, :], 1, 0).astype(bf16)
        gate = jnp.sum(jnp.where(hit, gates, 0.0), axis=1, keepdims=True)
        gs[rows, :] = jnp.broadcast_to(gate, (CAP, 128))
        kept = jnp.sum(jnp.where(slots > -0.5, 1, 0))
        offs[e, b] = off
        offs_out[e, b] = off
        off = off + (kept + 15) // 16 * 16
    offs_out[e, blocks] = off
    tail = pl.ds(pl.multiple_of(off, 16), TILE)
    xg[tail, :] = jnp.zeros((TILE, width), bf16)
    cg[tail, :] = jnp.zeros((TILE, width), bf16)
    gs[tail, :] = jnp.zeros((TILE, 128), f32)
    lane = lax.broadcasted_iota(jnp.int32, (TILE, SIDE), 1)

    def step(i, carry):
        rows = pl.ds(pl.multiple_of(i * TILE, TILE), TILE)
        w_gate = wg_ref[...].reshape(hid, width)
        w_up = wu_ref[...].reshape(hid, width)
        w_down = wd_ref[...].reshape(hid, width)
        x = xg[rows, :]
        c = cg[rows, :].astype(f32)
        gate = gs[rows, :][:, :1]
        gate_value = dot(x, w_gate, 1, 1)
        up_value = dot(x, w_up, 1, 1)
        sig = 1.0 / (1.0 + jnp.exp(-gate_value))
        silu = gate_value * sig
        active = (silu * up_value).astype(bf16)
        acts[rows, 2 * hid :] = active
        result = dot(active, w_down, 1, 0).astype(bf16).astype(f32)
        slope = jnp.sum(result * c, axis=1, keepdims=True)
        high = slope.astype(bf16).astype(f32)
        low = slope - high
        so[rows, :] = (gate * result).astype(bf16)
        pair_grad = (gate * c).astype(bf16)
        cg[rows, :] = pair_grad
        active_grad = dot(pair_grad, w_down, 1, 1)
        gate_back = (active_grad * up_value * (sig * (1.0 + gate_value * (1.0 - sig)))).astype(bf16)
        up_back = (active_grad * silu).astype(bf16)
        acts[rows, :hid] = gate_back
        acts[rows, hid : 2 * hid] = up_back
        for copy in tile_copies(i, e):
            copy.start()
        rg[e, rows, width:] = jnp.where(
            lane == expert, high, jnp.where(lane == expert + EXPERTS, low, 0.0)
        ).astype(bf16)
        rg[e, rows, :width] = (dot(gate_back, w_gate, 1, 0) + dot(up_back, w_up, 1, 0)).astype(bf16)
        return carry

    steps = pl.cdiv(off, TILE)
    lax.fori_loop(0, steps, step, 0)
    last[0] = steps
    rg[e, pl.ds(pl.multiple_of(steps * TILE, TILE), CAP), :] = jnp.zeros((CAP, width + SIDE), bf16)

    @pl.when(e == count - 1)
    def _():
        local_count = rg.shape[0]
        stores = []
        for b in range(blocks):
            picks = []
            for k in range(local_count):
                stage[b % 2, k * CAP : (k + 1) * CAP, :] = rg[
                    k, pl.ds(pl.multiple_of(offs[k, b], 16), CAP), :
                ]
                hit = slot_iota == s_t[b, pl.ds(base[0] + k, 1), :]
                picks.append(jnp.where(hit, 1.0, 0.0).astype(bf16))
            ob[b] = dot(jnp.concatenate(picks, 0), stage[b % 2], 0, 0).astype(bf16)
            stores.append(pltpu.make_async_copy(ob.at[b], rows_out[b], sems.at[b]))
            stores[b].start()
        wait_tiles(e)
        for store in stores:
            store.wait()


def expert_grad_body(first, offs, acts, xg, pg, out):
    e = pl.program_id(0) + first
    blocks = offs.shape[1] - 1
    steps = pl.cdiv(offs[e, blocks], TILE)
    parts, _, _, part, width = out.shape
    hid = parts * part

    @pl.when(steps == 0)
    def _():
        out[...] = jnp.zeros_like(out)

    for n in range(1, xg.shape[1] // TILE + 1):

        @pl.when(steps == n)
        def _(n=n):
            for i, right in enumerate((xg, xg, pg)):
                for h in range(parts):
                    at = i * hid + h * part
                    out[h, 0, i] = dot(
                        acts[0, : n * TILE, at : at + part], right[0, : n * TILE, :], 0, 0
                    ).astype(bf16)


def expert_sum_body(blocks, tokens, offs, so, slots, *refs):
    outs, stage = refs[:blocks], refs[blocks]
    local_count, width = so.shape[0], so.shape[2]
    slot_iota = lax.broadcasted_iota(jnp.int32, (CAP, tokens), 0).astype(f32)
    place = lax.broadcasted_iota(jnp.int32, (CAP, width), 0)
    for b in range(blocks):
        picks = []
        for k in range(local_count):
            off = pl.multiple_of(offs[k, b], 16)
            values = so[k, pl.ds(off, CAP), :]
            stage[b % 2, k * CAP : (k + 1) * CAP, :] = jnp.where(
                place < offs[k, blocks] - off, values.astype(f32), 0.0
            ).astype(bf16)
            picks.append(jnp.where(slot_iota == slots[k, b], 1.0, 0.0).astype(bf16))
        outs[b][...] = dot(jnp.concatenate(picks, 0), stage[b % 2], 0, 0).astype(bf16)


def expert_call(base, rows, grads, router, weights):
    hidden_parts, matrices, part, width = weights.shape
    local_count = matrices // 3
    blocks, tokens = len(rows), rows[0].shape[0]
    hid = hidden_parts * part
    most = blocks * CAP
    room = most + TILE

    def weight_spec(m):
        return pl.BlockSpec(
            (hidden_parts, 1, part, width), lambda e: (0, m * local_count + e, 0, 0)
        )

    got = pl.pallas_call(
        functools.partial(expert_body, blocks, tokens),
        grid=(local_count,),
        out_shape=[struct((tokens, width + SIDE))] * blocks
        + [
            struct((local_count, room, 3 * hid)),
            struct((local_count, room, width)),
            struct((local_count, room, width)),
            struct((local_count, room, width)),
            struct((local_count, blocks, 1, tokens), f32),
            struct((local_count, blocks + 1), jnp.int32),
        ],
        in_specs=[SMEM] + [ANY] * (2 * blocks) + [VMEM] + [weight_spec(m) for m in range(3)],
        out_specs=[ANY] * (blocks + 4)
        + [pl.BlockSpec((1, blocks, 1, tokens), lambda e: (e, 0, 0, 0)), SMEM],
        scratch_shapes=[
            pltpu.VMEM((blocks, tokens, width), bf16),
            pltpu.VMEM((blocks, tokens + EXPERTS, width), bf16),
            pltpu.VMEM((blocks, EXPERTS, tokens), f32),
            pltpu.VMEM((blocks, EXPERTS, tokens), f32),
            pltpu.VMEM((room, width), bf16),
            pltpu.VMEM((room, width), bf16),
            pltpu.VMEM((room, width), bf16),
            pltpu.VMEM((room, 3 * hid), bf16),
            pltpu.VMEM((room, 128), f32),
            pltpu.VMEM((local_count, room, width + SIDE), bf16),
            pltpu.VMEM((2, local_count * CAP, width + SIDE), bf16),
            pltpu.VMEM((blocks, tokens, width + SIDE), bf16),
            pltpu.SMEM((local_count, blocks), jnp.int32),
            pltpu.SMEM((1,), jnp.int32),
            pltpu.SemaphoreType.DMA((2 * blocks,)),
            pltpu.SemaphoreType.DMA((4, room // TILE)),
        ],
        compiler_params=pltpu.CompilerParams(vmem_limit_bytes=58 * MIB),
        cost_estimate=pl.CostEstimate(
            flops=10**6, bytes_accessed=10**4, transcendentals=0
        ),
        name="experts",
    )(base, *rows, *grads, router, weights, weights, weights)
    rows_back, (acts, xg, pg, so, slots, offs) = got[:blocks], got[blocks:]

    def grads_of(first, number, acts):
        return pl.pallas_call(
            functools.partial(expert_grad_body, first),
            grid=(number,),
            out_shape=struct((hidden_parts, number, 3, part, width)),
            in_specs=[SMEM]
            + [
                pl.BlockSpec((1, most, n), lambda e: (e + first, 0, 0))
                for n in (3 * hid, width, width)
            ],
            out_specs=pl.BlockSpec((hidden_parts, 1, 3, part, width), lambda e: (0, e, 0, 0, 0)),
            compiler_params=pltpu.CompilerParams(vmem_limit_bytes=48 * MIB),
            cost_estimate=pl.CostEstimate(flops=10**6, bytes_accessed=10**4, transcendentals=0),
            name="expert_grads",
        )(offs, acts, xg, pg)

    def outs_of(so):
        return call(
            functools.partial(expert_sum_body, blocks, tokens),
            [struct((tokens, width))] * blocks,
            (offs, so, slots),
            scratch=[pltpu.VMEM((2, local_count * CAP, width), bf16)],
            smem=1,
            name="expert_sum",
            flops=10**6,
            nbytes=10**4,
        )

    return rows_back, acts, so, grads_of, outs_of


def after(values, first):
    return lax.optimization_barrier((values, first))


def flip(values, axis, bit):
    n = lax.axis_size(axis)
    return lax.ppermute(values, axis, [(i, i ^ bit) for i in range(n)])


def gather_hidden(block):
    blocks, marks = [block], [0]
    bit = lax.axis_size("hidden") // 2
    while bit:
        blocks, marks = blocks + [flip(b, "hidden", bit) for b in blocks], marks + [m ^ bit for m in marks]
        bit //= 2
    return blocks, marks


def sum_hidden(keep):
    bit = 1
    n = lax.axis_size("hidden")
    while bit < n:
        far = {m: flip(keep[m], "hidden", bit) for m in keep if m & bit}
        near = {m: keep[m] for m in keep if not m & bit}
        if 2 * bit == n:
            return near[0], far[bit]
        keep = {m: (near[m].astype(f32) + far[m ^ bit].astype(f32)).astype(bf16) for m in near}
        bit *= 2


def shift(values, by):
    n = lax.axis_size("expert")
    return lax.ppermute(values, "expert", [(i, (i + 2 * by) % n) for i in range(n)])


def gather_expert(block, before=()):
    n = lax.axis_size("expert")
    if n != 8:
        whole = lax.all_gather(block, "expert", axis=0, tiled=False)
        return [whole[i] for i in range(n)], before
    side = flip(block, "expert", 1)
    up = shift(block, 1)
    down = shift(block, -1)
    up_after, (side, *before) = after(up, [side, *before])
    far = shift(up_after, 1)
    line = [up, far, down]
    return [block] + line + [side] + [flip(b, "expert", 1) for b in line], before


def take_add(near, got, first):
    n, rest = near.shape[0] // 2, near.shape[1:]
    spec = pl.BlockSpec((1,) + rest, lambda i: (2 * i + first,) + (0,) * len(rest))
    return pl.pallas_call(
        add_body,
        grid=(n,),
        out_shape=struct((n,) + rest),
        in_specs=[spec, spec],
        out_specs=pl.BlockSpec((1,) + rest, lambda i: (i,) + (0,) * len(rest)),
        compiler_params=pltpu.CompilerParams(vmem_limit_bytes=40 * MIB),
        cost_estimate=pl.CostEstimate(flops=10**6, bytes_accessed=10**4, transcendentals=0),
        name="take_add",
    )(near, got)


def sum_parts(near, far):
    return sum_parts_end(near, *sum_parts_begin(near, flip(far, "hidden", 1)))


def sum_parts_begin(near, got):
    return got, (take_add(near, got, 1) if got.shape[0] > 1 else None)


def sum_parts_end(near, got, far):
    bit = 2
    left = [near]
    while got.shape[0] > 1:
        if got.shape[0] > 2:
            near = take_add(near, got, 0)
            left = [near]
        else:
            left = [near[0], got[0]]
        got = flip(far, "hidden", bit)
        bit *= 2
        if got.shape[0] > 1:
            far = take_add(near, got, 1)
    return left, got[0]


def add_body(a, b, out):
    out[...] = (a[...].astype(f32) + b[...].astype(f32)).astype(bf16)


def add(a, b):
    return call(add_body, struct(a.shape), (a, b), name="add")


def sum_expert(parts):
    n = lax.axis_size("expert")
    if n != 8:
        return [
            lax.psum_scatter(jnp.concatenate(parts, 0), "expert", scatter_dimension=0, tiled=True)
        ]
    line = [None] * 4
    for k in (2, 1, 3, 0):
        line[k] = add(parts[k], flip(parts[4 + k], "expert", 1))
    near = add(line[1], shift(line[2], -1))
    return [line[0], shift(near, -1), shift(line[3], 1)]


def sum_expert_beside(parts, begin, works):
    flip_2 = flip(parts[6], "expert", 1)
    held = begin()
    flip_2, held = after(flip_2, held)
    far = add(parts[2], flip_2)

    far, held = works[0](far, held)
    side, _ = after(parts[5], flip_2)
    flip_1 = flip(side, "expert", 1)
    turn_1 = shift(far, -1)
    (flip_1, turn_1), held = after([flip_1, turn_1], held)
    near = add(add(parts[1], flip_1), turn_1)

    near, held = works[1](near, held)
    side, _ = after(parts[7], [flip_1, turn_1])
    flip_3 = flip(side, "expert", 1)
    result_a = shift(near, -1)
    (flip_3, result_a), held = after([flip_3, result_a], held)
    line_3 = add(parts[3], flip_3)

    line_3, held = works[2](line_3, held)
    side, _ = after(parts[4], [flip_3, result_a])
    flip_0 = flip(side, "expert", 1)
    result_b = shift(line_3, 1)
    (flip_0, result_b), held = after([flip_0, result_b], held)
    return [add(parts[0], flip_0), result_a, result_b], held


def local(
    inputs,
    first_gain,
    query_weight,
    key_weight,
    value_weight,
    out_weight,
    second_gain,
    router_weight,
    gate_weight,
    up_weight,
    down_weight,
    routes,
    segments,
    cotangent,
):
    tokens, width = inputs.shape
    hidden_index = lax.axis_index("hidden")
    expert_index = lax.axis_index("expert")
    groups = lax.axis_size("expert")
    hidden_parts = lax.axis_size("hidden")
    local_count = gate_weight.shape[0]
    gain_one, gain_two = first_gain[None, :], second_gain[None, :]
    router = jnp.pad(router_weight, ((0, 0), (0, SIDE - EXPERTS)))
    spectrum = rope_base ** (-jnp.arange(HEAD_DIM // 2, dtype=f32) * 2.0 / HEAD_DIM)
    me = hidden_index.astype(jnp.int32).reshape(1)

    grad_rows = call(
        route_body,
        struct((tokens + EXPERTS, width)),
        (routes, cotangent),
        name="route",
        flops=10**6,
        nbytes=10**4,
    )
    grads, _ = gather_expert(grad_rows)
    kv, normed, cosine, sine = call(
        project_kv_body,
        (
            struct((tokens, 2 * KV + SIDE)),
            struct((tokens, width)),
            struct((tokens, 128), f32),
            struct((tokens, 128), f32),
        ),
        (
            me * tokens,
            inputs,
            gain_one,
            key_weight,
            value_weight,
            jnp.tile(spectrum, 4)[None, :],
            segments[None, :],
        ),
        smem=1,
        name="project_kv",
        flops=10**6,
        nbytes=10**4,
    )
    q = call(
        project_q_body,
        struct((tokens, width)),
        (normed, query_weight, cosine, sine),
        name="project_q",
        flops=10**6,
        nbytes=10**4,
    )
    kvs, marks = gather_hidden(kv)
    nb = len(kvs)
    weights = jnp.concatenate([gate_weight, up_weight, down_weight], axis=0)
    weights, (kvs[1], grads[1], grads[4]) = after(weights, [kvs[1], grads[1], grads[4]])
    weights_all = lax.all_gather(weights, "hidden", axis=0, tiled=False)
    places = jnp.stack([(hidden_index ^ m) * tokens for m in marks]).astype(jnp.int32)
    hidden, ffn, att, lse, gates = call(
        functools.partial(attend_body, nb),
        (
            struct((tokens, width), f32),
            struct((tokens, width)),
            struct((tokens, width)),
            struct((tokens, 128), f32),
            struct((tokens, SIDE), f32),
        ),
        (places, inputs, q, *kvs, out_weight, gain_two, router, routes),
        scratch=[pltpu.VMEM((nb, tokens, tokens), f32)],
        smem=1,
        name="attend",
        flops=10**6,
        nbytes=10**4,
    )
    if groups == 8:
        first = [1, 2, 3, 4, 5, 7]
        ffn_out, held = after(ffn, [grads[i] for i in first])
        for i, g in zip(first, held):
            grads[i] = g
        rows, (grads[6],) = gather_expert(ffn_out, (grads[6],))
    else:
        rows, _ = gather_expert(ffn)

    first_expert = (expert_index * local_count).astype(jnp.int32)
    rows_back, todo = [], []
    chunk = min(CHUNK, groups)
    router_rows = router_weight.T
    for i in range(0, groups, chunk):
        r, *rest = expert_call(
            first_expert.reshape(1),
            rows[i : i + chunk],
            grads[i : i + chunk],
            router_rows,
            weights_all,
        )
        rows_back += r
        todo.append(rest)
    half_count = (local_count + 1) // 2

    def weight_grads(first, number, held):
        parts = [grads_of(first, number, a) for (_, _, grads_of, _), a in zip(todo, held)]
        return parts[0] if len(parts) == 1 else sum(p.astype(f32) for p in parts).astype(bf16)

    def matrix_sum(part):
        return lax.psum_scatter(part, "hidden", scatter_dimension=0, tiled=False)

    def token_sums(held):
        return [o for (_, _, _, outs_of), so in zip(todo, held) for o in outs_of(so)]

    all_acts, all_so = [t[0] for t in todo], [t[1] for t in todo]
    rest_count = local_count - half_count
    if groups == 8 and rest_count:

        def begin():
            return weight_grads(0, half_count, all_acts)

        def work_2(values, held):
            dw_halves.append(matrix_sum(held))
            values, acts = after(values, all_acts)
            return values, weight_grads(half_count, rest_count, acts)

        def work_3(values, held):
            dw_halves.append(matrix_sum(held))
            values, so = after(values, all_so)
            return values, token_sums(so)

        dw_halves = []
        row_parts, outs = sum_expert_beside(
            rows_back, begin, (work_2, work_3, lambda values, held: (values, held))
        )
        row_parts[0], outs = after(row_parts[0], outs)
    else:
        row_parts = sum_expert(rows_back)
        dw_halves = [matrix_sum(weight_grads(0, local_count, all_acts))]
        outs = token_sums(all_so)

    hidden_grad, branch, logit_grad, gain_share, out_grad = call(
        functools.partial(hidden_back_body, len(row_parts)),
        (
            struct((tokens, width), f32),
            struct((tokens, width)),
            struct((tokens, SIDE)),
            struct((tokens, width)),
            struct((tokens, width)),
        ),
        (*row_parts, hidden, gates, cotangent, gain_two, router, out_weight),
        name="hidden_back",
    )

    def weight_parts(left, right, sides=()):
        n = right.shape[1] + (SIDE if sides else 0)
        rows_each = width // groups // hidden_parts
        shape = (hidden_parts // 2, groups, rows_each, n)
        return call(
            functools.partial(weight_body, groups, hidden_parts, len(sides)),
            (struct(shape), struct(shape)),
            (me, left, right, *[v for pair in sides for v in pair]),
            scratch=[pltpu.VMEM((hidden_parts, groups, rows_each, n), bf16)],
            smem=1,
            name="weight_grad",
        )

    def sum_over_mesh(near, got, far):
        left, got = sum_parts_end(near, got, far)
        half = sum([v.astype(f32) for v in left], got.astype(f32)).astype(bf16)
        got = lax.all_to_all(half, "expert", split_axis=0, concat_axis=0, tiled=True)
        return jnp.sum(got.astype(f32), axis=0)

    def across(near, far):
        return (near, *sum_parts_begin(near, flip(far, "hidden", 1)))

    spot = jnp.broadcast_to(
        (jnp.arange(SIDE, dtype=jnp.int32) == EXPERTS).astype(bf16)[None, :], (tokens, SIDE)
    )
    first_parts = weight_parts(att, branch, ((ffn, logit_grad), (gain_share, spot)))
    first_parts = across(*first_parts)
    out_grad, first_parts = after(out_grad, first_parts)
    first_sums = sum_over_mesh(*first_parts)
    dq, *dkvs = call(
        functools.partial(attention_back_body, nb),
        [struct((tokens, width))] + [struct((tokens, 2 * KV))] * nb,
        (places, out_grad, q, *kvs, lse, cosine, sine),
        scratch=[pltpu.VMEM((nb, tokens, tokens), f32)],
        smem=1,
        name="attention_back",
    )
    ka, kb = sum_hidden(dict(zip(marks, dkvs)))
    dw_sum = jnp.concatenate(dw_halves, 0).astype(f32)
    query_near, query_got, query_far = across(*weight_parts(normed, dq))
    query_far, kb = after(query_far, kb)
    query_sum = sum_over_mesh(query_near, query_got, query_far)
    input_grad, dkv, gain_share_one = call(
        finish_body,
        (struct((tokens, width)), struct((tokens, 2 * KV)), struct((tokens, width))),
        (
            ka,
            kb,
            dq,
            query_weight,
            key_weight,
            value_weight,
            hidden_grad,
            inputs,
            gain_one,
            cosine,
            sine,
        ),
        name="finish",
        flops=10**6,
        nbytes=10**4,
    )
    last_sums = sum_over_mesh(*across(*weight_parts(normed, dkv, ((gain_share_one, spot),))))
    moe = sum_expert(outs)
    block_out = (hidden + sum(m.astype(f32) for m in moe)).astype(bf16)
    return (
        block_out,
        input_grad,
        last_sums[:, 2 * KV + EXPERTS],
        query_sum,
        last_sums[:, :KV],
        last_sums[:, KV : 2 * KV],
        first_sums[:, :width],
        first_sums[:, width + EXPERTS],
        first_sums[:, width : width + EXPERTS],
        dw_sum[:, 0],
        dw_sum[:, 1],
        dw_sum[:, 2],
    )


def solution(mesh):
    tokens = P(("expert", "hidden"), None)
    flat = P(("expert", "hidden"))
    units = P("expert", "hidden", None)
    in_specs = (tokens,) + (P(),) * 7 + (units,) * 3 + (tokens, flat, tokens)
    out_specs = (tokens, tokens, flat) + (tokens,) * 4 + (flat, tokens) + (units,) * 3
    return jax.shard_map(local, mesh=mesh, in_specs=in_specs, out_specs=out_specs, check_vma=False)
```

```python
import functools

import jax
import jax.numpy as jnp
from jax import lax
from jax.experimental import pallas as pl
from jax.experimental.pallas import tpu as pltpu
from jax.sharding import PartitionSpec as P

HEADS = 16
KV_HEADS = 8
HEAD_DIM = 64
EXPERTS = 32
CAP = 128
KV = KV_HEADS * HEAD_DIM
SIDE = 128
TILE = 256
CHUNK = 8

epsilon = 1e-06
rope_base = 10000.0
masked_score = -1e30
bf16 = jnp.bfloat16
f32 = jnp.float32
ANY = pl.BlockSpec(memory_space=pl.ANY)
SMEM = pl.BlockSpec(memory_space=pltpu.SMEM)
VMEM = pl.BlockSpec(memory_space=pltpu.VMEM)
MIB = 1024 * 1024


def dot(a, b, ca, cb):
    return lax.dot_general(a, b, (((ca,), (cb,)), ((), ())), preferred_element_type=f32)


def rms(values):
    return lax.rsqrt(jnp.mean(values * values, axis=-1, keepdims=True) + epsilon)


def norm_back(grad, values, gain):
    q = rms(values)
    w = grad * gain
    back = q * w - values * (q * q * q) * jnp.mean(w * values, axis=-1, keepdims=True)
    return back, grad * values * q


def turn(u, cosine, sine):
    lane = lax.broadcasted_iota(jnp.int32, u.shape, 1)
    half = HEAD_DIM // 2
    partner = jnp.where(
        lane % HEAD_DIM < half, pltpu.roll(u, 2 * HEAD_DIM - half, 1), pltpu.roll(u, half, 1)
    )
    return u * cosine + partner * sine


def struct(shape, dtype=bf16):
    return jax.ShapeDtypeStruct(shape, dtype)


def call(body, outs, ins, scratch=(), smem=0, name=None, mib=20, flops=10**6, nbytes=10**4):
    return pl.pallas_call(
        body,
        out_shape=outs,
        in_specs=[SMEM] * smem + [VMEM] * (len(ins) - smem),
        out_specs=jax.tree.map(lambda _: VMEM, outs),
        scratch_shapes=list(scratch),
        compiler_params=pltpu.CompilerParams(vmem_limit_bytes=mib * MIB),
        cost_estimate=pl.CostEstimate(flops=flops, bytes_accessed=nbytes, transcendentals=0),
        name=name,
    )(*ins)


def route_body(routes, cot, out):
    tokens, width = cot.shape
    lane = lax.broadcasted_iota(jnp.int32, (tokens, 128), 1)
    named = jnp.zeros((tokens, 128), f32)
    for i in range(routes.shape[1]):
        named = named + jnp.where(lane == routes[:, i : i + 1], 1.0, 0.0)
    row = lax.broadcasted_iota(jnp.int32, (tokens, tokens), 0)
    col = lax.broadcasted_iota(jnp.int32, (tokens, tokens), 1)
    earlier = dot(jnp.where(row > col, 1.0, 0.0).astype(bf16), named.astype(bf16), 1, 0)
    code = jnp.where(named > 0.0, jnp.where(earlier < CAP, earlier, -1.0), -2.0)
    out[:tokens, :] = cot[...]
    out[tokens:, :tokens] = code.T[:EXPERTS].astype(bf16)
    out[tokens:, tokens:] = jnp.zeros((EXPERTS, width - tokens), bf16)


def project_kv_body(place, x, gain, wk, wv, spectrum, seg, kv_out, n_out, c_out, s_out):
    tokens = x.shape[0]
    source = x[...].astype(f32)
    normed = (source * rms(source) * gain[...]).astype(bf16)
    n_out[...] = normed
    at = lax.broadcasted_iota(jnp.int32, (tokens, 128), 0) + place[0]
    lane = lax.broadcasted_iota(jnp.int32, (tokens, 128), 1)
    angles = at.astype(f32) * spectrum[...]
    c = jnp.cos(angles)
    s = jnp.sin(angles)
    s = jnp.where(lane % HEAD_DIM < HEAD_DIM // 2, -s, s)
    c_out[...] = c
    s_out[...] = s
    k = dot(normed, wk[...], 1, 0)
    for i in range(0, KV, 128):
        kv_out[:, i : i + 128] = turn(k[:, i : i + 128], c, s).astype(bf16)
    kv_out[:, KV : 2 * KV] = dot(normed, wv[...], 1, 0).astype(bf16)
    kv_out[:, 2 * KV :] = jnp.broadcast_to(seg[...].astype(f32), (SIDE, tokens)).T.astype(bf16)


def project_q_body(normed, wq, c, s, q_out):
    q = dot(normed[...], wq[...], 1, 0)
    for i in range(0, q.shape[1], 128):
        turned = turn(q[:, i : i + 128], c[...], s[...]).astype(bf16)
        q_out[:, i : i + 128] = turned * bf16(HEAD_DIM**-0.5)


def fill_bias(places, kvs, bias):
    tokens = kvs[0].shape[0]
    mine = kvs[0][:, 2 * KV :].astype(f32)[:, :1]
    row = lax.broadcasted_iota(jnp.int32, (tokens, tokens), 0) + places[0]
    col = lax.broadcasted_iota(jnp.int32, (tokens, tokens), 1)
    for b, kv in enumerate(kvs):
        theirs = kv[:, 2 * KV :].astype(f32).T[:1, :]
        keep = (mine == theirs) & (col + places[b] <= row)
        bias[b] = jnp.where(keep, 0.0, masked_score)


def pair_rows(values, j):
    return jnp.concatenate(
        [values[:, 128 * j : 128 * j + HEAD_DIM], values[:, 128 * j + HEAD_DIM : 128 * j + 128]], 0
    )


def pair_columns(values, tokens):
    return jnp.concatenate([values[:tokens], values[tokens:]], 1)


def scores_of(q2, kv, bias, j):
    tokens = kv.shape[0]
    s = dot(q2, kv[:, HEAD_DIM * j : HEAD_DIM * (j + 1)], 1, 1)
    return (s.reshape(2, tokens, tokens) + bias[None]).reshape(2 * tokens, tokens)


def attend_body(
    nb, places, x, q, *refs
):
    kvs, (wo, gain, router, routes, hid_out, ffn_out, att_out, lse_out, gates_out, bias) = (
        refs[:nb],
        refs[nb:],
    )
    tokens = x.shape[0]
    fill_bias(places, kvs, bias)
    lane = lax.broadcasted_iota(jnp.int32, (tokens, 128), 1)
    lse = jnp.zeros((tokens, 128), f32)
    for j in range(KV_HEADS):
        q2 = pair_rows(q, j)
        s = [scores_of(q2, kv, bias[b], j) for b, kv in enumerate(kvs)]
        peak = functools.reduce(
            jnp.maximum, [jnp.max(t, axis=1, keepdims=True) for t in s]
        )
        p = [jnp.exp(t - peak) for t in s]
        total = sum(jnp.sum(t, axis=1, keepdims=True) for t in p)
        o = sum(
            dot(t.astype(bf16), kv[:, KV + HEAD_DIM * j : KV + HEAD_DIM * (j + 1)], 1, 0)
            for t, kv in zip(p, kvs)
        )
        att_out[:, 128 * j : 128 * j + 128] = pair_columns(o / total, tokens).astype(bf16)
        log_total = peak + jnp.log(total)
        lse = jnp.where(lane == 2 * j, log_total[:tokens], lse)
        lse = jnp.where(lane == 2 * j + 1, log_total[tokens:], lse)
    lse_out[...] = lse
    hidden = x[...].astype(f32) + dot(att_out[...], wo[...], 1, 0)
    hid_out[...] = hidden
    ffn = (hidden * rms(hidden) * gain[...]).astype(bf16)
    ffn_out[...] = ffn
    lane = lax.broadcasted_iota(jnp.int32, (tokens, SIDE), 1)
    named = jnp.zeros((tokens, SIDE), f32)
    for i in range(routes.shape[1]):
        named = named + jnp.where(lane == routes[:, i : i + 1], 1.0, 0.0)
    gates_out[...] = gates_of(dot(ffn, router[...], 1, 0), named, 1)


def gates_of(logits, named, axis):
    logits = jnp.where(named > 0.0, logits, masked_score)
    peak = jnp.max(logits, axis=axis, keepdims=True)
    raised = jnp.where(named > 0.0, jnp.exp(logits - peak), 0.0)
    return raised / jnp.sum(raised, axis=axis, keepdims=True)


def hidden_back_body(
    n, *refs
):
    row_sum = sum(r[...].astype(f32) for r in refs[:n])
    (hid, gates, cot, gain, router, wo, hgrad_out, branch_out, lg_out, gp_out, do_out) = refs[n:]
    width = hid.shape[1]
    side = row_sum[:, width:]
    lane = lax.broadcasted_iota(jnp.int32, side.shape, 1)
    slopes = jnp.where(lane < EXPERTS, side + pltpu.roll(side, SIDE - EXPERTS, 1), 0.0)
    g = gates[...]
    logit_grad = (g * (slopes - jnp.sum(g * slopes, axis=1, keepdims=True))).astype(bf16)
    lg_out[...] = logit_grad
    ffn_grad = row_sum[:, :width] + dot(logit_grad, router[...], 1, 1)
    back, share = norm_back(ffn_grad, hid[...], gain[...])
    gp_out[...] = share.astype(bf16)
    hidden_grad = cot[...].astype(f32) + back
    hgrad_out[...] = hidden_grad
    branch = hidden_grad.astype(bf16)
    branch_out[...] = branch
    do_out[...] = dot(branch, wo[...], 1, 1).astype(bf16)


def attention_back_body(marks, places, do_s, q, *refs):
    nb = len(marks)
    kvs = refs[:nb]
    (lse, cosine, sine, dq_out, near, far, bias) = refs[nb:]
    dkv = [(far if m % 2 else near).at[m // 2] for m in marks]
    tokens = q.shape[0]
    fill_bias(places, kvs, bias)
    c, s = cosine[...], sine[...]
    for j in range(KV_HEADS):
        q2 = pair_rows(q, j)
        do2 = pair_rows(do_s, j)
        lse2 = jnp.concatenate([lse[:, 2 * j : 2 * j + 1], lse[:, 2 * j + 1 : 2 * j + 2]], 0)
        p, dp = [], []
        inner = jnp.zeros((2 * tokens, 1), f32)
        for b, kv in enumerate(kvs):
            pb = jnp.exp(scores_of(q2, kv, bias[b], j) - lse2)
            db = dot(do2, kv[:, KV + HEAD_DIM * j : KV + HEAD_DIM * (j + 1)], 1, 1)
            inner = inner + jnp.sum(pb * db, axis=1, keepdims=True)
            p.append(pb)
            dp.append(db)
        dq2 = jnp.zeros((2 * tokens, HEAD_DIM), f32)
        for b, kv in enumerate(kvs):
            ds = (p[b] * (dp[b] - inner)).astype(bf16)
            dq2 = dq2 + dot(ds, kv[:, HEAD_DIM * j : HEAD_DIM * (j + 1)], 1, 0)
            dkv[b][:, HEAD_DIM * j : HEAD_DIM * (j + 1)] = dot(ds, q2, 0, 0).astype(bf16)
            dkv[b][:, KV + HEAD_DIM * j : KV + HEAD_DIM * (j + 1)] = dot(
                p[b].astype(bf16), do2, 0, 0
            ).astype(bf16)
        dq = pair_columns(dq2, tokens) * HEAD_DIM**-0.5
        dq_out[:, 128 * j : 128 * j + 128] = turn(dq, c, -s).astype(bf16)


def finish_body(
    near, got, far, dq, wq, wk, wv, hgrad, x, gain, cosine, sine, in_out, dkv_out, gp_out
):
    total = near[0].astype(f32) + got[0].astype(f32) + far[0].astype(f32)
    c, s = cosine[...], sine[...]
    for at in range(0, KV, 128):
        dkv_out[:, at : at + 128] = turn(total[:, at : at + 128], c, -s).astype(bf16)
    dkv_out[:, KV:] = total[:, KV:].astype(bf16)
    grad = dot(dq[...], wq[...], 1, 1)
    grad = grad + dot(dkv_out[:, :KV], wk[...], 1, 1) + dot(dkv_out[:, KV:], wv[...], 1, 1)
    back, share = norm_back(grad, x[...].astype(f32), gain[...])
    gp_out[...] = share.astype(bf16)
    in_out[...] = (hgrad[...] + back).astype(bf16)


def weight_body(groups, parts, n_side, me, left, right, *refs):
    sides, (near, far, held) = refs[: 2 * n_side], refs[2 * n_side :]
    width = right.shape[1]

    def put(values, lo, hi):
        v = values.reshape(groups, parts, -1, hi - lo)
        for h in range(parts):
            held[h, :, :, lo:hi] = v[:, h].astype(bf16)

    for at in range(0, width, 512):
        put(dot(left[...], right[:, at : at + 512], 0, 0), at, at + 512)
    if n_side:
        put(
            sum(dot(sides[2 * i][...], sides[2 * i + 1][...], 0, 0) for i in range(n_side)),
            width,
            width + SIDE,
        )
    for m in range(parts):
        (far if m % 2 else near)[m // 2] = held[me[0] ^ m]


def expert_body(blocks, tokens, base, *refs):
    xs, cs = refs[:blocks], refs[blocks : 2 * blocks]
    router, wg_ref, wu_ref, wd_ref = refs[2 * blocks : 2 * blocks + 4]
    refs = refs[2 * blocks + 4 :]
    rows_out = refs[:blocks]
    acts_out, x_out, pg_out, so_out, slots_out, offs_out = refs[blocks : blocks + 6]
    (x_s, c_s, g_t, s_t, xg, cg, so, acts, gs, rg, stage, ob, offs, last, sems, tile_sems) = refs[
        blocks + 6 :
    ]
    e = pl.program_id(0)
    count = pl.num_programs(0)
    width = x_s.shape[2]
    hid = acts.shape[1] // 3
    slot_iota = lax.broadcasted_iota(jnp.int32, (CAP, tokens), 0).astype(f32)
    expert = base[0] + e

    def loads(b):
        return (
            pltpu.make_async_copy(xs[b], x_s.at[b], sems.at[b]),
            pltpu.make_async_copy(cs[b], c_s.at[b], sems.at[blocks + b]),
        )

    def tile_copies(i, at):
        rows = pl.ds(pl.multiple_of(i * TILE, TILE), TILE)
        pairs = ((acts, acts_out), (xg, x_out), (cg, pg_out), (so, so_out))
        return [
            pltpu.make_async_copy(a.at[rows, :], o.at[at, rows, :], tile_sems.at[n, i])
            for n, (a, o) in enumerate(pairs)
        ]

    def wait_tiles(at):
        def wait_one(i, carry):
            for copy in tile_copies(i, at):
                copy.wait()
            return carry

        lax.fori_loop(0, last[0], wait_one, 0)

    @pl.when(e == 0)
    def _():
        for b in range(blocks):
            for load in loads(b):
                load.start()

    @pl.when(e > 0)
    def _():
        wait_tiles(e - 1)

    off = jnp.int32(0)
    for b in range(blocks):

        @pl.when(e == 0)
        def _(b=b):
            for load in loads(b):
                load.wait()
            code = c_s[b, tokens:, :tokens].astype(f32)
            s_t[b] = code
            g_t[b] = gates_of(
                dot(router[...], x_s[b], 1, 1), jnp.where(code > -1.5, 1.0, 0.0), 0
            )

        off = pl.multiple_of(off, 16)
        rows = pl.ds(off, CAP)
        mine = pl.ds(expert, 1)
        slots, gates = s_t[b, mine, :], g_t[b, mine, :]
        slots_out[0, b] = slots
        hit = slot_iota == slots
        pick = jnp.where(hit, 1.0, 0.0).astype(bf16)
        xg[rows, :] = dot(pick, x_s[b], 1, 0).astype(bf16)
        cg[rows, :] = dot(pick, c_s[b, :tokens, :], 1, 0).astype(bf16)
        gate = jnp.sum(jnp.where(hit, gates, 0.0), axis=1, keepdims=True)
        gs[rows, :] = jnp.broadcast_to(gate, (CAP, 128))
        kept = jnp.sum(jnp.where(slots > -0.5, 1, 0))
        offs[e, b] = off
        offs_out[e, b] = off
        off = off + (kept + 15) // 16 * 16
    offs_out[e, blocks] = off
    tail = pl.ds(pl.multiple_of(off, 16), TILE)
    xg[tail, :] = jnp.zeros((TILE, width), bf16)
    cg[tail, :] = jnp.zeros((TILE, width), bf16)
    gs[tail, :] = jnp.zeros((TILE, 128), f32)
    lane = lax.broadcasted_iota(jnp.int32, (TILE, SIDE), 1)

    def step(i, carry):
        rows = pl.ds(pl.multiple_of(i * TILE, TILE), TILE)
        w_gate = wg_ref[...].reshape(hid, width)
        w_up = wu_ref[...].reshape(hid, width)
        w_down = wd_ref[...].reshape(hid, width)
        x = xg[rows, :]
        c = cg[rows, :].astype(f32)
        gate = gs[rows, :][:, :1]
        gate_value = dot(x, w_gate, 1, 1)
        up_value = dot(x, w_up, 1, 1)
        sig = 1.0 / (1.0 + jnp.exp(-gate_value))
        silu = gate_value * sig
        active = (silu * up_value).astype(bf16)
        acts[rows, 2 * hid :] = active
        result = dot(active, w_down, 1, 0).astype(bf16).astype(f32)
        slope = jnp.sum(result * c, axis=1, keepdims=True)
        high = slope.astype(bf16).astype(f32)
        low = slope - high
        so[rows, :] = (gate * result).astype(bf16)
        pair_grad = (gate * c).astype(bf16)
        cg[rows, :] = pair_grad
        active_grad = dot(pair_grad, w_down, 1, 1)
        gate_back = (active_grad * up_value * (sig * (1.0 + gate_value * (1.0 - sig)))).astype(bf16)
        up_back = (active_grad * silu).astype(bf16)
        acts[rows, :hid] = gate_back
        acts[rows, hid : 2 * hid] = up_back
        for copy in tile_copies(i, e):
            copy.start()
        rg[e, rows, width:] = jnp.where(
            lane == expert, high, jnp.where(lane == expert + EXPERTS, low, 0.0)
        ).astype(bf16)
        rg[e, rows, :width] = (dot(gate_back, w_gate, 1, 0) + dot(up_back, w_up, 1, 0)).astype(bf16)
        return carry

    steps = pl.cdiv(off, TILE)
    lax.fori_loop(0, steps, step, 0)
    last[0] = steps
    rg[e, pl.ds(pl.multiple_of(steps * TILE, TILE), CAP), :] = jnp.zeros((CAP, width + SIDE), bf16)

    @pl.when(e == count - 1)
    def _():
        local_count = rg.shape[0]
        stores = []
        for b in range(blocks):
            picks = []
            for k in range(local_count):
                stage[b % 2, k * CAP : (k + 1) * CAP, :] = rg[
                    k, pl.ds(pl.multiple_of(offs[k, b], 16), CAP), :
                ]
                hit = slot_iota == s_t[b, pl.ds(base[0] + k, 1), :]
                picks.append(jnp.where(hit, 1.0, 0.0).astype(bf16))
            ob[b] = dot(jnp.concatenate(picks, 0), stage[b % 2], 0, 0).astype(bf16)
            stores.append(pltpu.make_async_copy(ob.at[b], rows_out[b], sems.at[b]))
            stores[b].start()
        wait_tiles(e)
        for store in stores:
            store.wait()


def expert_grad_body(first, offs, acts, xg, pg, out):
    e = pl.program_id(0) + first
    blocks = offs.shape[1] - 1
    steps = pl.cdiv(offs[e, blocks], TILE)
    parts, _, _, part, width = out.shape
    hid = parts * part

    @pl.when(steps == 0)
    def _():
        out[...] = jnp.zeros_like(out)

    for n in range(1, xg.shape[1] // TILE + 1):

        @pl.when(steps == n)
        def _(n=n):
            for i, right in enumerate((xg, xg, pg)):
                for h in range(parts):
                    at = i * hid + h * part
                    out[h, 0, i] = dot(
                        acts[0, : n * TILE, at : at + part], right[0, : n * TILE, :], 0, 0
                    ).astype(bf16)


def expert_grad_split_body(first, me, offs, acts, xg, pg, near, far):
    e = pl.program_id(0) + first
    blocks = offs.shape[1] - 1
    steps = pl.cdiv(offs[e, blocks], TILE)
    half, _, _, part, width = near.shape
    hid = 2 * half * part

    @pl.when(steps == 0)
    def _():
        near[...] = jnp.zeros_like(near)
        far[...] = jnp.zeros_like(far)

    for n in range(1, xg.shape[1] // TILE + 1):

        @pl.when(steps == n)
        def _(n=n):
            for i, right in enumerate((xg, xg, pg)):
                for p in range(half):
                    for out, place in ((near, me[0] % 2), (far, 1 - me[0] % 2)):
                        at = pl.multiple_of(i * hid + (2 * p + place) * part, part)
                        out[p, 0, i] = dot(
                            acts[0, : n * TILE, pl.ds(at, part)], right[0, : n * TILE, :], 0, 0
                        ).astype(bf16)


def expert_sum_body(blocks, tokens, offs, so, slots, *refs):
    outs, stage = refs[:blocks], refs[blocks]
    local_count, width = so.shape[0], so.shape[2]
    slot_iota = lax.broadcasted_iota(jnp.int32, (CAP, tokens), 0).astype(f32)
    place = lax.broadcasted_iota(jnp.int32, (CAP, width), 0)
    for b in range(blocks):
        picks = []
        for k in range(local_count):
            off = pl.multiple_of(offs[k, b], 16)
            values = so[k, pl.ds(off, CAP), :]
            stage[b % 2, k * CAP : (k + 1) * CAP, :] = jnp.where(
                place < offs[k, blocks] - off, values.astype(f32), 0.0
            ).astype(bf16)
            picks.append(jnp.where(slot_iota == slots[k, b], 1.0, 0.0).astype(bf16))
        outs[b][...] = dot(jnp.concatenate(picks, 0), stage[b % 2], 0, 0).astype(bf16)


def expert_call(me, base, rows, grads, router, weights):
    hidden_parts, matrices, part, width = weights.shape
    local_count = matrices // 3
    blocks, tokens = len(rows), rows[0].shape[0]
    hid = hidden_parts * part
    most = blocks * CAP
    room = most + TILE

    def weight_spec(m):
        return pl.BlockSpec(
            (hidden_parts, 1, part, width), lambda e: (0, m * local_count + e, 0, 0)
        )

    got = pl.pallas_call(
        functools.partial(expert_body, blocks, tokens),
        grid=(local_count,),
        out_shape=[struct((tokens, width + SIDE))] * blocks
        + [
            struct((local_count, room, 3 * hid)),
            struct((local_count, room, width)),
            struct((local_count, room, width)),
            struct((local_count, room, width)),
            struct((local_count, blocks, 1, tokens), f32),
            struct((local_count, blocks + 1), jnp.int32),
        ],
        in_specs=[SMEM] + [ANY] * (2 * blocks) + [VMEM] + [weight_spec(m) for m in range(3)],
        out_specs=[ANY] * (blocks + 4)
        + [pl.BlockSpec((1, blocks, 1, tokens), lambda e: (e, 0, 0, 0)), SMEM],
        scratch_shapes=[
            pltpu.VMEM((blocks, tokens, width), bf16),
            pltpu.VMEM((blocks, tokens + EXPERTS, width), bf16),
            pltpu.VMEM((blocks, EXPERTS, tokens), f32),
            pltpu.VMEM((blocks, EXPERTS, tokens), f32),
            pltpu.VMEM((room, width), bf16),
            pltpu.VMEM((room, width), bf16),
            pltpu.VMEM((room, width), bf16),
            pltpu.VMEM((room, 3 * hid), bf16),
            pltpu.VMEM((room, 128), f32),
            pltpu.VMEM((local_count, room, width + SIDE), bf16),
            pltpu.VMEM((2, local_count * CAP, width + SIDE), bf16),
            pltpu.VMEM((blocks, tokens, width + SIDE), bf16),
            pltpu.SMEM((local_count, blocks), jnp.int32),
            pltpu.SMEM((1,), jnp.int32),
            pltpu.SemaphoreType.DMA((2 * blocks,)),
            pltpu.SemaphoreType.DMA((4, room // TILE)),
        ],
        compiler_params=pltpu.CompilerParams(vmem_limit_bytes=58 * MIB),
        cost_estimate=pl.CostEstimate(
            flops=10**6, bytes_accessed=10**4, transcendentals=0
        ),
        name="experts",
    )(base, *rows, *grads, router, weights, weights, weights)
    rows_back, (acts, xg, pg, so, slots, offs) = got[:blocks], got[blocks:]

    def grads_of(first, number, acts):
        return pl.pallas_call(
            functools.partial(expert_grad_body, first),
            grid=(number,),
            out_shape=struct((hidden_parts, number, 3, part, width)),
            in_specs=[SMEM]
            + [
                pl.BlockSpec((1, most, n), lambda e: (e + first, 0, 0))
                for n in (3 * hid, width, width)
            ],
            out_specs=pl.BlockSpec((hidden_parts, 1, 3, part, width), lambda e: (0, e, 0, 0, 0)),
            compiler_params=pltpu.CompilerParams(vmem_limit_bytes=60 * MIB),
            cost_estimate=pl.CostEstimate(flops=10**6, bytes_accessed=10**4, transcendentals=0),
            name="expert_grads",
        )(offs, acts, xg, pg)

    def split_grads_of(first, number, acts):
        shape = (hidden_parts // 2, number, 3, part, width)
        out_spec = pl.BlockSpec((hidden_parts // 2, 1, 3, part, width), lambda e: (0, e, 0, 0, 0))
        return pl.pallas_call(
            functools.partial(expert_grad_split_body, first),
            grid=(number,),
            out_shape=(struct(shape), struct(shape)),
            in_specs=[SMEM, SMEM]
            + [
                pl.BlockSpec((1, most, n), lambda e: (e + first, 0, 0))
                for n in (3 * hid, width, width)
            ],
            out_specs=(out_spec, out_spec),
            compiler_params=pltpu.CompilerParams(vmem_limit_bytes=60 * MIB),
            cost_estimate=pl.CostEstimate(flops=10**6, bytes_accessed=10**4, transcendentals=0),
            name="expert_grads",
        )(me, offs, acts, xg, pg)

    def outs_of(so):
        return call(
            functools.partial(expert_sum_body, blocks, tokens),
            [struct((tokens, width))] * blocks,
            (offs, so, slots),
            scratch=[pltpu.VMEM((2, local_count * CAP, width), bf16)],
            smem=1,
            name="expert_sum",
            mib=60,
            flops=10**6,
            nbytes=10**4,
        )

    return rows_back, acts, so, grads_of, split_grads_of, outs_of


def after(values, first):
    return lax.optimization_barrier((values, first))


def flip(values, axis, bit):
    n = lax.axis_size(axis)
    return lax.ppermute(values, axis, [(i, i ^ bit) for i in range(n)])


def gather_hidden(block):
    blocks, marks = [block], [0]
    bit = lax.axis_size("hidden") // 2
    while bit:
        blocks, marks = blocks + [flip(b, "hidden", bit) for b in blocks], marks + [m ^ bit for m in marks]
        bit //= 2
    return blocks, marks


def sum_hidden(keep):
    bit = 1
    n = lax.axis_size("hidden")
    while bit < n:
        far = {m: flip(keep[m], "hidden", bit) for m in keep if m & bit}
        near = {m: keep[m] for m in keep if not m & bit}
        if 2 * bit == n:
            return near[0], far[bit]
        keep = {m: (near[m].astype(f32) + far[m ^ bit].astype(f32)).astype(bf16) for m in near}
        bit *= 2


def shift(values, by):
    n = lax.axis_size("expert")
    return lax.ppermute(values, "expert", [(i, (i + 2 * by) % n) for i in range(n)])


def gather_expert(block, before=()):
    n = lax.axis_size("expert")
    if n != 8:
        whole = lax.all_gather(block, "expert", axis=0, tiled=False)
        return [whole[i] for i in range(n)], before
    side = flip(block, "expert", 1)
    up = shift(block, 1)
    down = shift(block, -1)
    up_after, (side, *before) = after(up, [side, *before])
    far = shift(up_after, 1)
    line = [up, far, down]
    return [block] + line + [side] + [flip(b, "expert", 1) for b in line], before


def take_add(near, got, first):
    n, rest = near.shape[0] // 2, near.shape[1:]
    spec = pl.BlockSpec((1,) + rest, lambda i: (2 * i + first,) + (0,) * len(rest))
    return pl.pallas_call(
        add_body,
        grid=(n,),
        out_shape=struct((n,) + rest),
        in_specs=[spec, spec],
        out_specs=pl.BlockSpec((1,) + rest, lambda i: (i,) + (0,) * len(rest)),
        compiler_params=pltpu.CompilerParams(vmem_limit_bytes=10 * MIB),
        cost_estimate=pl.CostEstimate(flops=10**6, bytes_accessed=10**4, transcendentals=0),
        name="take_add",
    )(near, got)


def all_add(a, b):
    rest = a.shape[1:]
    spec = pl.BlockSpec((1,) + rest, lambda i: (i,) + (0,) * len(rest))
    return pl.pallas_call(
        add_body,
        grid=(a.shape[0],),
        out_shape=struct(a.shape),
        in_specs=[spec, spec],
        out_specs=spec,
        compiler_params=pltpu.CompilerParams(vmem_limit_bytes=60 * MIB),
        cost_estimate=pl.CostEstimate(flops=10**6, bytes_accessed=10**4, transcendentals=0),
        name="all_add",
    )(a, b)


def sum_parts(near, far):
    return sum_parts_end(near, *sum_parts_begin(near, flip(far, "hidden", 1)))


def sum_parts_begin(near, got):
    return got, (take_add(near, got, 1) if got.shape[0] > 1 else None)


def sum_parts_end(near, got, far):
    bit = 2
    left = [near]
    while got.shape[0] > 1:
        if got.shape[0] > 2:
            near = take_add(near, got, 0)
            left = [near]
        else:
            left = [near[0], got[0]]
        got = flip(far, "hidden", bit)
        bit *= 2
        if got.shape[0] > 1:
            far = take_add(near, got, 1)
    return left, got[0]


def add_body(a, b, out):
    out[...] = (a[...].astype(f32) + b[...].astype(f32)).astype(bf16)


def add(a, b):
    return call(add_body, struct(a.shape), (a, b), name="add", mib=6)


def sum_expert(parts):
    n = lax.axis_size("expert")
    if n != 8:
        return [
            lax.psum_scatter(jnp.concatenate(parts, 0), "expert", scatter_dimension=0, tiled=True)
        ]
    line = [None] * 4
    for k in (2, 1, 3, 0):
        line[k] = add(parts[k], flip(parts[4 + k], "expert", 1))
    near = add(line[1], shift(line[2], -1))
    return [line[0], shift(near, -1), shift(line[3], 1)]


def sum_expert_beside(parts, begin, works):
    flip_2 = flip(parts[6], "expert", 1)
    held = begin()
    flip_2, held = after(flip_2, held)
    far = add(parts[2], flip_2)

    far, held = works[0](far, held)
    side, _ = after(parts[5], flip_2)
    flip_1 = flip(side, "expert", 1)
    turn_1 = shift(far, -1)
    (flip_1, turn_1), held = after([flip_1, turn_1], held)
    near = add(add(parts[1], flip_1), turn_1)

    near, held = works[1](near, held)
    side, _ = after(parts[7], [flip_1, turn_1])
    flip_3 = flip(side, "expert", 1)
    result_a = shift(near, -1)
    (flip_3, result_a), held = after([flip_3, result_a], held)
    line_3 = add(parts[3], flip_3)

    line_3, held = works[2](line_3, held)
    side, _ = after(parts[4], [flip_3, result_a])
    flip_0 = flip(side, "expert", 1)
    result_b = shift(line_3, 1)
    (flip_0, result_b), held = after([flip_0, result_b], held)
    return [add(parts[0], flip_0), result_a, result_b], held


def local(
    inputs,
    first_gain,
    query_weight,
    key_weight,
    value_weight,
    out_weight,
    second_gain,
    router_weight,
    gate_weight,
    up_weight,
    down_weight,
    routes,
    segments,
    cotangent,
):
    tokens, width = inputs.shape
    hidden_index = lax.axis_index("hidden")
    expert_index = lax.axis_index("expert")
    groups = lax.axis_size("expert")
    hidden_parts = lax.axis_size("hidden")
    local_count = gate_weight.shape[0]
    gain_one, gain_two = first_gain[None, :], second_gain[None, :]
    router = jnp.pad(router_weight, ((0, 0), (0, SIDE - EXPERTS)))
    spectrum = rope_base ** (-jnp.arange(HEAD_DIM // 2, dtype=f32) * 2.0 / HEAD_DIM)
    me = hidden_index.astype(jnp.int32).reshape(1)

    grad_rows = call(
        route_body,
        struct((tokens + EXPERTS, width)),
        (routes, cotangent),
        name="route",
        flops=10**6,
        nbytes=10**4,
    )
    grads, _ = gather_expert(grad_rows)
    kv, normed, cosine, sine = call(
        project_kv_body,
        (
            struct((tokens, 2 * KV + SIDE)),
            struct((tokens, width)),
            struct((tokens, 128), f32),
            struct((tokens, 128), f32),
        ),
        (
            me * tokens,
            inputs,
            gain_one,
            key_weight,
            value_weight,
            jnp.tile(spectrum, 4)[None, :],
            segments[None, :],
        ),
        smem=1,
        name="project_kv",
        flops=10**6,
        nbytes=10**4,
    )
    q = call(
        project_q_body,
        struct((tokens, width)),
        (normed, query_weight, cosine, sine),
        name="project_q",
        flops=10**6,
        nbytes=10**4,
    )
    kvs, marks = gather_hidden(kv)
    nb = len(kvs)
    weights = jnp.concatenate([gate_weight, up_weight, down_weight], axis=0)
    weights, (kvs[1], grads[1], grads[4]) = after(weights, [kvs[1], grads[1], grads[4]])
    weights_all = lax.all_gather(weights, "hidden", axis=0, tiled=False)
    places = jnp.stack([(hidden_index ^ m) * tokens for m in marks]).astype(jnp.int32)
    hidden, ffn, att, lse, gates = call(
        functools.partial(attend_body, nb),
        (
            struct((tokens, width), f32),
            struct((tokens, width)),
            struct((tokens, width)),
            struct((tokens, 128), f32),
            struct((tokens, SIDE), f32),
        ),
        (places, inputs, q, *kvs, out_weight, gain_two, router, routes),
        scratch=[pltpu.VMEM((nb, tokens, tokens), f32)],
        smem=1,
        name="attend",
        flops=10**6,
        nbytes=10**4,
    )
    if groups == 8:
        first = [1, 2, 3, 4, 5, 7]
        ffn_out, held = after(ffn, [grads[i] for i in first])
        for i, g in zip(first, held):
            grads[i] = g
        rows, (grads[6],) = gather_expert(ffn_out, (grads[6],))
    else:
        rows, _ = gather_expert(ffn)

    first_expert = (expert_index * local_count).astype(jnp.int32)
    rows_back, todo = [], []
    chunk = min(CHUNK, groups)
    router_rows = router_weight.T
    for i in range(0, groups, chunk):
        r, *rest = expert_call(
            me,
            first_expert.reshape(1),
            rows[i : i + chunk],
            grads[i : i + chunk],
            router_rows,
            weights_all,
        )
        rows_back += r
        todo.append(rest)
    half_count = (local_count + 1) // 2

    def weight_grads(first, number, held):
        parts = [grads_of(first, number, a) for (_, _, grads_of, _, _), a in zip(todo, held)]
        return parts[0] if len(parts) == 1 else sum(p.astype(f32) for p in parts).astype(bf16)

    def matrix_sum(part):
        return lax.psum_scatter(part, "hidden", scatter_dimension=0, tiled=False)

    pairs = [[c + 2 * i for i in range(hidden_parts // 2)] for c in range(2)]

    def token_sums(held):
        return [o for (_, _, _, _, outs_of), so in zip(todo, held) for o in outs_of(so)]

    all_acts, all_so = [t[0] for t in todo], [t[1] for t in todo]
    rest_count = local_count - half_count
    if groups == 8 and rest_count:

        def begin():
            return weight_grads(0, half_count, all_acts)

        def work_2(values, held):
            dw_halves.append(matrix_sum(held))
            values, acts = after(values, all_acts)
            return values, todo[0][3](half_count, rest_count, acts[0])

        def work_3(values, held):
            values, so = after(values, all_so)
            return values, (held, token_sums(so))

        dw_halves = []
        row_parts, (dw_rest, outs) = sum_expert_beside(
            rows_back, begin, (work_2, work_3, lambda values, held: (values, held))
        )
        row_parts[0], outs = after(row_parts[0], outs)
    else:
        row_parts = sum_expert(rows_back)
        dw_halves = [matrix_sum(weight_grads(0, local_count, all_acts))]
        outs, dw_rest = token_sums(all_so), None

    hidden_grad, branch, logit_grad, gain_share, out_grad = call(
        functools.partial(hidden_back_body, len(row_parts)),
        (
            struct((tokens, width), f32),
            struct((tokens, width)),
            struct((tokens, SIDE)),
            struct((tokens, width)),
            struct((tokens, width)),
        ),
        (*row_parts, hidden, gates, cotangent, gain_two, router, out_weight),
        name="hidden_back",
    )

    def across(near, far):
        return (near, *sum_parts_begin(near, flip(far, "hidden", 1)))

    def weight_parts(left, right, sides=()):
        n = right.shape[1] + (SIDE if sides else 0)
        rows_each = width // groups // hidden_parts
        shape = (hidden_parts // 2, groups, rows_each, n)
        return call(
            functools.partial(weight_body, groups, hidden_parts, len(sides)),
            (struct(shape), struct(shape)),
            (me, left, right, *[v for pair in sides for v in pair]),
            scratch=[pltpu.VMEM((hidden_parts, groups, rows_each, n), bf16)],
            smem=1,
            name="weight_grad",
        )

    def end_over_mesh(left, got):
        half = sum([v.astype(f32) for v in left], got.astype(f32)).astype(bf16)
        got = lax.all_to_all(half, "expert", split_axis=0, concat_axis=0, tiled=True)
        return jnp.sum(got.astype(f32), axis=0)

    spot = jnp.broadcast_to(
        (jnp.arange(SIDE, dtype=jnp.int32) == EXPERTS).astype(bf16)[None, :], (tokens, SIDE)
    )
    first_parts = weight_parts(att, branch, ((ffn, logit_grad), (gain_share, spot)))
    first_parts = across(*first_parts)
    out_grad, first_parts = after(out_grad, first_parts)
    first_left, first_got = sum_parts_end(*first_parts)
    dq, near, far = call(
        functools.partial(attention_back_body, marks),
        (
            struct((tokens, width)),
            struct((nb // 2, tokens, 2 * KV)),
            struct((nb // 2, tokens, 2 * KV)),
        ),
        (places, out_grad, q, *kvs, lse, cosine, sine),
        scratch=[pltpu.VMEM((nb, tokens, tokens), f32)],
        smem=1,
        name="attention_back",
    )
    if groups == 8:
        moe = [flip(o, "expert", 1) for o in outs[4:]]
        far, (first_got, moe[1], moe[2]) = after(far, [first_got, moe[1], moe[2]])
        moved = shift(add(outs[2], moe[2]), -1)
    kv_near, kv_got, kv_far = across(near, far)
    kb = flip(kv_far, "hidden", 2)
    dq, kv_far = after(dq, kv_far)
    query_near, query_got, query_far = across(*weight_parts(normed, dq))
    kb, query_far = after(kb, query_far)
    query_left, query_got = sum_parts_end(query_near, query_got, query_far)
    if dw_rest is not None:
        near, far = dw_rest
        kv_far, far = after(kv_far, far)
        dw_rest = all_add(near, flip(far, "hidden", 1))
        kb, dw_rest = after(kb, dw_rest)
        dw_rest, dw_halves[0] = after(dw_rest, dw_halves[0])
        dw_halves.append(
            lax.psum_scatter(
                dw_rest, "hidden", scatter_dimension=0, axis_index_groups=pairs, tiled=False
            )
        )
    dw_sum = jnp.concatenate(dw_halves, 0).astype(f32)
    input_grad, dkv, gain_share_one = call(
        finish_body,
        (struct((tokens, width)), struct((tokens, 2 * KV)), struct((tokens, width))),
        (
            kv_near,
            kv_got,
            kb,
            dq,
            query_weight,
            key_weight,
            value_weight,
            hidden_grad,
            inputs,
            gain_one,
            cosine,
            sine,
        ),
        name="finish",
        mib=60,
        flops=10**6,
        nbytes=10**4,
    )
    last_near, last_got, last_far = across(*weight_parts(normed, dkv, ((gain_share_one, spot),)))
    if groups == 8:
        last_far, (moe[0], moe[3], moved) = after(last_far, [moe[0], moe[3], moved])
        near = add(add(outs[1], moe[1]), moved)
        moe = [add(outs[0], moe[0]), shift(near, -1), shift(add(outs[3], moe[3]), 1)]
    else:
        moe = sum_expert(outs)
    first_sums = end_over_mesh(first_left, first_got)
    query_sum = end_over_mesh(query_left, query_got)
    last_left, last_got = sum_parts_end(last_near, last_got, last_far)
    last_got, (first_sums, query_sum) = after(last_got, [first_sums, query_sum])
    half = sum([v.astype(f32) for v in last_left], last_got.astype(f32)).astype(bf16)
    got = lax.all_to_all(half, "expert", split_axis=0, concat_axis=0, tiled=True)
    block_out = (hidden + sum(m.astype(f32) for m in moe)).astype(bf16)
    got, (block_out, dw_out) = after(got, [block_out, [dw_sum[:, i] for i in range(3)]])
    last_sums = jnp.sum(got.astype(f32), axis=0)
    return (
        block_out,
        input_grad,
        last_sums[:, 2 * KV + EXPERTS],
        query_sum,
        last_sums[:, :KV],
        last_sums[:, KV : 2 * KV],
        first_sums[:, :width],
        first_sums[:, width + EXPERTS],
        first_sums[:, width : width + EXPERTS],
        *dw_out,
    )


def solution(mesh):
    tokens = P(("expert", "hidden"), None)
    flat = P(("expert", "hidden"))
    units = P("expert", "hidden", None)
    in_specs = (tokens,) + (P(),) * 7 + (units,) * 3 + (tokens, flat, tokens)
    out_specs = (tokens, tokens, flat) + (tokens,) * 4 + (flat, tokens) + (units,) * 3
    return jax.shard_map(local, mesh=mesh, in_specs=in_specs, out_specs=out_specs, check_vma=False)
```

```python
import functools

import jax
import jax.numpy as jnp
from jax import lax
from jax.experimental import pallas as pl
from jax.experimental.pallas import tpu as pltpu
from jax.sharding import PartitionSpec as P

HEADS = 16
KV_HEADS = 8
HEAD_DIM = 64
EXPERTS = 32
CAP = 128
KV = KV_HEADS * HEAD_DIM
SIDE = 128
TILE = 256
CHUNK = 8

epsilon = 1e-06
rope_base = 10000.0
masked_score = -1e30
bf16 = jnp.bfloat16
f32 = jnp.float32
ANY = pl.BlockSpec(memory_space=pl.ANY)
SMEM = pl.BlockSpec(memory_space=pltpu.SMEM)
VMEM = pl.BlockSpec(memory_space=pltpu.VMEM)
MIB = 1024 * 1024


def dot(a, b, ca, cb):
    return lax.dot_general(a, b, (((ca,), (cb,)), ((), ())), preferred_element_type=f32)


def rms(values):
    return lax.rsqrt(jnp.mean(values * values, axis=-1, keepdims=True) + epsilon)


def norm_back(grad, values, gain):
    q = rms(values)
    w = grad * gain
    back = q * w - values * (q * q * q) * jnp.mean(w * values, axis=-1, keepdims=True)
    return back, grad * values * q


def turn(u, cosine, sine):
    lane = lax.broadcasted_iota(jnp.int32, u.shape, 1)
    half = HEAD_DIM // 2
    partner = jnp.where(
        lane % HEAD_DIM < half, pltpu.roll(u, 2 * HEAD_DIM - half, 1), pltpu.roll(u, half, 1)
    )
    return u * cosine + partner * sine


def struct(shape, dtype=bf16):
    return jax.ShapeDtypeStruct(shape, dtype)


def call(body, outs, ins, scratch=(), smem=0, name=None, mib=20, flops=10**6, nbytes=10**4):
    return pl.pallas_call(
        body,
        out_shape=outs,
        in_specs=[SMEM] * smem + [VMEM] * (len(ins) - smem),
        out_specs=jax.tree.map(lambda _: VMEM, outs),
        scratch_shapes=list(scratch),
        compiler_params=pltpu.CompilerParams(vmem_limit_bytes=mib * MIB),
        cost_estimate=pl.CostEstimate(flops=flops, bytes_accessed=nbytes, transcendentals=0),
        name=name,
    )(*ins)


def route_body(routes, cot, out):
    tokens, width = cot.shape
    lane = lax.broadcasted_iota(jnp.int32, (tokens, 128), 1)
    named = jnp.zeros((tokens, 128), f32)
    for i in range(routes.shape[1]):
        named = named + jnp.where(lane == routes[:, i : i + 1], 1.0, 0.0)
    row = lax.broadcasted_iota(jnp.int32, (tokens, tokens), 0)
    col = lax.broadcasted_iota(jnp.int32, (tokens, tokens), 1)
    earlier = dot(jnp.where(row > col, 1.0, 0.0).astype(bf16), named.astype(bf16), 1, 0)
    code = jnp.where(named > 0.0, jnp.where(earlier < CAP, earlier, -1.0), -2.0)
    out[:tokens, :] = cot[...]
    rows = code.T.astype(bf16)
    half = EXPERTS // 2
    out[tokens:, :tokens] = rows[:half]
    out[tokens:, tokens : 2 * tokens] = rows[half:EXPERTS]
    out[tokens:, 2 * tokens :] = jnp.zeros((half, width - 2 * tokens), bf16)


def project_kv_body(place, x, gain, wk, wv, spectrum, seg, kv_out, n_out, c_out, s_out):
    tokens = x.shape[0]
    source = x[...].astype(f32)
    normed = (source * rms(source) * gain[...]).astype(bf16)
    n_out[...] = normed
    at = lax.broadcasted_iota(jnp.int32, (tokens, 128), 0) + place[0]
    lane = lax.broadcasted_iota(jnp.int32, (tokens, 128), 1)
    angles = at.astype(f32) * spectrum[...]
    c = jnp.cos(angles)
    s = jnp.sin(angles)
    s = jnp.where(lane % HEAD_DIM < HEAD_DIM // 2, -s, s)
    c_out[...] = c
    s_out[...] = s
    k = dot(normed, wk[...], 1, 0)
    for i in range(0, KV, 128):
        kv_out[:, i : i + 128] = turn(k[:, i : i + 128], c, s).astype(bf16)
    kv_out[:, KV : 2 * KV] = dot(normed, wv[...], 1, 0).astype(bf16)
    kv_out[:, 2 * KV :] = jnp.broadcast_to(seg[...].astype(f32), (SIDE, tokens)).T.astype(bf16)


def project_q_body(normed, wq, c, s, q_out):
    q = dot(normed[...], wq[...], 1, 0)
    for i in range(0, q.shape[1], 128):
        turned = turn(q[:, i : i + 128], c[...], s[...]).astype(bf16)
        q_out[:, i : i + 128] = turned * bf16(HEAD_DIM**-0.5)


def fill_bias(places, kvs, bias):
    tokens = kvs[0].shape[0]
    mine = kvs[0][:, 2 * KV :].astype(f32)[:, :1]
    row = lax.broadcasted_iota(jnp.int32, (tokens, tokens), 0) + places[0]
    col = lax.broadcasted_iota(jnp.int32, (tokens, tokens), 1)
    for b, kv in enumerate(kvs):
        theirs = kv[:, 2 * KV :].astype(f32).T[:1, :]
        keep = (mine == theirs) & (col + places[b] <= row)
        bias[b] = jnp.where(keep, 0.0, masked_score)


def pair_rows(values, j):
    return jnp.concatenate(
        [values[:, 128 * j : 128 * j + HEAD_DIM], values[:, 128 * j + HEAD_DIM : 128 * j + 128]], 0
    )


def pair_columns(values, tokens):
    return jnp.concatenate([values[:tokens], values[tokens:]], 1)


def scores_of(q2, kv, bias, j):
    tokens = kv.shape[0]
    s = dot(q2, kv[:, HEAD_DIM * j : HEAD_DIM * (j + 1)], 1, 1)
    return (s.reshape(2, tokens, tokens) + bias[None]).reshape(2 * tokens, tokens)


def attend_body(
    nb, places, x, q, *refs
):
    kvs, (wo, gain, router, routes, hid_out, ffn_out, att_out, lse_out, gates_out, bias) = (
        refs[:nb],
        refs[nb:],
    )
    tokens = x.shape[0]
    fill_bias(places, kvs, bias)
    lane = lax.broadcasted_iota(jnp.int32, (tokens, 128), 1)
    lse = jnp.zeros((tokens, 128), f32)
    for j in range(KV_HEADS):
        q2 = pair_rows(q, j)
        s = [scores_of(q2, kv, bias[b], j) for b, kv in enumerate(kvs)]
        peak = functools.reduce(
            jnp.maximum, [jnp.max(t, axis=1, keepdims=True) for t in s]
        )
        p = [jnp.exp(t - peak) for t in s]
        total = sum(jnp.sum(t, axis=1, keepdims=True) for t in p)
        o = sum(
            dot(t.astype(bf16), kv[:, KV + HEAD_DIM * j : KV + HEAD_DIM * (j + 1)], 1, 0)
            for t, kv in zip(p, kvs)
        )
        att_out[:, 128 * j : 128 * j + 128] = pair_columns(o / total, tokens).astype(bf16)
        log_total = peak + jnp.log(total)
        lse = jnp.where(lane == 2 * j, log_total[:tokens], lse)
        lse = jnp.where(lane == 2 * j + 1, log_total[tokens:], lse)
    lse_out[...] = lse
    hidden = x[...].astype(f32) + dot(att_out[...], wo[...], 1, 0)
    hid_out[...] = hidden
    ffn = (hidden * rms(hidden) * gain[...]).astype(bf16)
    ffn_out[...] = ffn
    lane = lax.broadcasted_iota(jnp.int32, (tokens, SIDE), 1)
    named = jnp.zeros((tokens, SIDE), f32)
    for i in range(routes.shape[1]):
        named = named + jnp.where(lane == routes[:, i : i + 1], 1.0, 0.0)
    gates_out[...] = gates_of(dot(ffn, router[...], 1, 0), named, 1)


def gates_of(logits, named, axis):
    logits = jnp.where(named > 0.0, logits, masked_score)
    peak = jnp.max(logits, axis=axis, keepdims=True)
    raised = jnp.where(named > 0.0, jnp.exp(logits - peak), 0.0)
    return raised / jnp.sum(raised, axis=axis, keepdims=True)


def hidden_back_body(
    n, *refs
):
    row_sum = sum(r[...].astype(f32) for r in refs[:n])
    (hid, gates, cot, gain, router, wo, hgrad_out, branch_out, lg_out, gp_out, do_out) = refs[n:]
    width = hid.shape[1]
    side = row_sum[:, width:]
    lane = lax.broadcasted_iota(jnp.int32, side.shape, 1)
    slopes = jnp.where(lane < EXPERTS, side + pltpu.roll(side, SIDE - EXPERTS, 1), 0.0)
    g = gates[...]
    logit_grad = (g * (slopes - jnp.sum(g * slopes, axis=1, keepdims=True))).astype(bf16)
    lg_out[...] = logit_grad
    ffn_grad = row_sum[:, :width] + dot(logit_grad, router[...], 1, 1)
    back, share = norm_back(ffn_grad, hid[...], gain[...])
    gp_out[...] = share.astype(bf16)
    hidden_grad = cot[...].astype(f32) + back
    hgrad_out[...] = hidden_grad
    branch = hidden_grad.astype(bf16)
    branch_out[...] = branch
    do_out[...] = dot(branch, wo[...], 1, 1).astype(bf16)


def attention_back_body(marks, places, do_s, q, *refs):
    nb = len(marks)
    kvs = refs[:nb]
    (lse, cosine, sine, dq_out, near, far, bias) = refs[nb:]
    dkv = [(far if m % 2 else near).at[m // 2] for m in marks]
    tokens = q.shape[0]
    fill_bias(places, kvs, bias)
    c, s = cosine[...], sine[...]
    for j in range(KV_HEADS):
        q2 = pair_rows(q, j)
        do2 = pair_rows(do_s, j)
        lse2 = jnp.concatenate([lse[:, 2 * j : 2 * j + 1], lse[:, 2 * j + 1 : 2 * j + 2]], 0)
        p, dp = [], []
        inner = jnp.zeros((2 * tokens, 1), f32)
        for b, kv in enumerate(kvs):
            pb = jnp.exp(scores_of(q2, kv, bias[b], j) - lse2)
            db = dot(do2, kv[:, KV + HEAD_DIM * j : KV + HEAD_DIM * (j + 1)], 1, 1)
            inner = inner + jnp.sum(pb * db, axis=1, keepdims=True)
            p.append(pb)
            dp.append(db)
        dq2 = jnp.zeros((2 * tokens, HEAD_DIM), f32)
        for b, kv in enumerate(kvs):
            ds = (p[b] * (dp[b] - inner)).astype(bf16)
            dq2 = dq2 + dot(ds, kv[:, HEAD_DIM * j : HEAD_DIM * (j + 1)], 1, 0)
            dkv[b][:, HEAD_DIM * j : HEAD_DIM * (j + 1)] = dot(ds, q2, 0, 0).astype(bf16)
            dkv[b][:, KV + HEAD_DIM * j : KV + HEAD_DIM * (j + 1)] = dot(
                p[b].astype(bf16), do2, 0, 0
            ).astype(bf16)
        dq = pair_columns(dq2, tokens) * HEAD_DIM**-0.5
        dq_out[:, 128 * j : 128 * j + 128] = turn(dq, c, -s).astype(bf16)


def finish_body(
    near, got, far, dq, wq, wk, wv, hgrad, x, gain, cosine, sine, in_out, dkv_out, gp_out
):
    total = near[0].astype(f32) + got[0].astype(f32) + far[0].astype(f32)
    c, s = cosine[...], sine[...]
    for at in range(0, KV, 128):
        dkv_out[:, at : at + 128] = turn(total[:, at : at + 128], c, -s).astype(bf16)
    dkv_out[:, KV:] = total[:, KV:].astype(bf16)
    grad = dot(dq[...], wq[...], 1, 1)
    grad = grad + dot(dkv_out[:, :KV], wk[...], 1, 1) + dot(dkv_out[:, KV:], wv[...], 1, 1)
    back, share = norm_back(grad, x[...].astype(f32), gain[...])
    gp_out[...] = share.astype(bf16)
    in_out[...] = (hgrad[...] + back).astype(bf16)


def weight_body(groups, parts, n_side, me, left, right, *refs):
    sides, (near, far, held) = refs[: 2 * n_side], refs[2 * n_side :]
    width = right.shape[1]

    def put(values, lo, hi):
        v = values.reshape(groups, parts, -1, hi - lo)
        for h in range(parts):
            held[h, :, :, lo:hi] = v[:, h].astype(bf16)

    for at in range(0, width, 512):
        put(dot(left[...], right[:, at : at + 512], 0, 0), at, at + 512)
    if n_side:
        put(
            sum(dot(sides[2 * i][...], sides[2 * i + 1][...], 0, 0) for i in range(n_side)),
            width,
            width + SIDE,
        )
    for m in range(parts):
        (far if m % 2 else near)[m // 2] = held[me[0] ^ m]


def expert_body(blocks, tokens, base, *refs):
    xs, cs = refs[:blocks], refs[blocks : 2 * blocks]
    router, wg_ref, wu_ref, wd_ref = refs[2 * blocks : 2 * blocks + 4]
    refs = refs[2 * blocks + 4 :]
    rows_out = refs[:blocks]
    acts_out, x_out, pg_out, so_out, slots_out, offs_out = refs[blocks : blocks + 6]
    (x_s, c_s, g_t, s_t, xg, cg, so, acts, gs, rg, stage, ob, offs, last, sems, tile_sems) = refs[
        blocks + 6 :
    ]
    e = pl.program_id(0)
    count = pl.num_programs(0)
    width = x_s.shape[2]
    hid = acts.shape[1] // 3
    slot_iota = lax.broadcasted_iota(jnp.int32, (CAP, tokens), 0).astype(f32)
    expert = base[0] + e

    def loads(b):
        return (
            pltpu.make_async_copy(xs[b], x_s.at[b], sems.at[b]),
            pltpu.make_async_copy(cs[b], c_s.at[b], sems.at[blocks + b]),
        )

    def tile_copies(i, at):
        rows = pl.ds(pl.multiple_of(i * TILE, TILE), TILE)
        pairs = ((acts, acts_out), (xg, x_out), (cg, pg_out), (so, so_out))
        return [
            pltpu.make_async_copy(a.at[rows, :], o.at[at, rows, :], tile_sems.at[n, i])
            for n, (a, o) in enumerate(pairs)
        ]

    def wait_tiles(at):
        def wait_one(i, carry):
            for copy in tile_copies(i, at):
                copy.wait()
            return carry

        lax.fori_loop(0, last[0], wait_one, 0)

    @pl.when(e == 0)
    def _():
        for b in range(blocks):
            for load in loads(b):
                load.start()

    @pl.when(e > 0)
    def _():
        wait_tiles(e - 1)

    off = jnp.int32(0)
    for b in range(blocks):

        @pl.when(e == 0)
        def _(b=b):
            for load in loads(b):
                load.wait()
            code = jnp.concatenate(
                [c_s[b, tokens:, :tokens], c_s[b, tokens:, tokens : 2 * tokens]], 0
            ).astype(f32)
            s_t[b] = code
            g_t[b] = gates_of(
                dot(router[...], x_s[b], 1, 1), jnp.where(code > -1.5, 1.0, 0.0), 0
            )

        off = pl.multiple_of(off, 16)
        rows = pl.ds(off, CAP)
        mine = pl.ds(expert, 1)
        slots, gates = s_t[b, mine, :], g_t[b, mine, :]
        slots_out[0, b] = slots
        hit = slot_iota == slots
        pick = jnp.where(hit, 1.0, 0.0).astype(bf16)
        xg[rows, :] = dot(pick, x_s[b], 1, 0).astype(bf16)
        cg[rows, :] = dot(pick, c_s[b, :tokens, :], 1, 0).astype(bf16)
        gate = jnp.sum(jnp.where(hit, gates, 0.0), axis=1, keepdims=True)
        gs[rows, :] = jnp.broadcast_to(gate, (CAP, 128))
        kept = jnp.sum(jnp.where(slots > -0.5, 1, 0))
        offs[e, b] = off
        offs_out[e, b] = off
        off = off + (kept + 15) // 16 * 16
    offs_out[e, blocks] = off
    tail = pl.ds(pl.multiple_of(off, 16), TILE)
    xg[tail, :] = jnp.zeros((TILE, width), bf16)
    cg[tail, :] = jnp.zeros((TILE, width), bf16)
    gs[tail, :] = jnp.zeros((TILE, 128), f32)
    lane = lax.broadcasted_iota(jnp.int32, (TILE, SIDE), 1)

    def step(i, carry):
        rows = pl.ds(pl.multiple_of(i * TILE, TILE), TILE)
        w_gate = wg_ref[...].reshape(hid, width)
        w_up = wu_ref[...].reshape(hid, width)
        w_down = wd_ref[...].reshape(hid, width)
        x = xg[rows, :]
        c = cg[rows, :].astype(f32)
        gate = gs[rows, :][:, :1]
        gate_value = dot(x, w_gate, 1, 1)
        up_value = dot(x, w_up, 1, 1)
        sig = 1.0 / (1.0 + jnp.exp(-gate_value))
        silu = gate_value * sig
        active = (silu * up_value).astype(bf16)
        acts[rows, 2 * hid :] = active
        result = dot(active, w_down, 1, 0).astype(bf16).astype(f32)
        slope = jnp.sum(result * c, axis=1, keepdims=True)
        high = slope.astype(bf16).astype(f32)
        low = slope - high
        so[rows, :] = (gate * result).astype(bf16)
        pair_grad = (gate * c).astype(bf16)
        cg[rows, :] = pair_grad
        active_grad = dot(pair_grad, w_down, 1, 1)
        gate_back = (active_grad * up_value * (sig * (1.0 + gate_value * (1.0 - sig)))).astype(bf16)
        up_back = (active_grad * silu).astype(bf16)
        acts[rows, :hid] = gate_back
        acts[rows, hid : 2 * hid] = up_back
        for copy in tile_copies(i, e):
            copy.start()
        rg[e, rows, width:] = jnp.where(
            lane == expert, high, jnp.where(lane == expert + EXPERTS, low, 0.0)
        ).astype(bf16)
        rg[e, rows, :width] = (dot(gate_back, w_gate, 1, 0) + dot(up_back, w_up, 1, 0)).astype(bf16)
        return carry

    steps = pl.cdiv(off, TILE)
    lax.fori_loop(0, steps, step, 0)
    last[0] = steps
    rg[e, pl.ds(pl.multiple_of(steps * TILE, TILE), CAP), :] = jnp.zeros((CAP, width + SIDE), bf16)

    @pl.when(e == count - 1)
    def _():
        local_count = rg.shape[0]
        stores = []
        for b in range(blocks):
            picks = []
            for k in range(local_count):
                stage[b % 2, k * CAP : (k + 1) * CAP, :] = rg[
                    k, pl.ds(pl.multiple_of(offs[k, b], 16), CAP), :
                ]
                hit = slot_iota == s_t[b, pl.ds(base[0] + k, 1), :]
                picks.append(jnp.where(hit, 1.0, 0.0).astype(bf16))
            ob[b] = dot(jnp.concatenate(picks, 0), stage[b % 2], 0, 0).astype(bf16)
            stores.append(pltpu.make_async_copy(ob.at[b], rows_out[b], sems.at[b]))
            stores[b].start()
        wait_tiles(e)
        for store in stores:
            store.wait()


def expert_grad_body(first, offs, acts, xg, pg, out):
    e = pl.program_id(0) + first
    blocks = offs.shape[1] - 1
    steps = pl.cdiv(offs[e, blocks], TILE)
    parts, _, _, part, width = out.shape
    hid = parts * part

    @pl.when(steps == 0)
    def _():
        out[...] = jnp.zeros_like(out)

    for n in range(1, xg.shape[1] // TILE + 1):

        @pl.when(steps == n)
        def _(n=n):
            for i, right in enumerate((xg, xg, pg)):
                for h in range(parts):
                    at = i * hid + h * part
                    out[h, 0, i] = dot(
                        acts[0, : n * TILE, at : at + part], right[0, : n * TILE, :], 0, 0
                    ).astype(bf16)


def expert_grad_split_body(first, me, offs, acts, xg, pg, near, far):
    e = pl.program_id(0) + first
    blocks = offs.shape[1] - 1
    steps = pl.cdiv(offs[e, blocks], TILE)
    half, _, _, part, width = near.shape
    hid = 2 * half * part

    @pl.when(steps == 0)
    def _():
        near[...] = jnp.zeros_like(near)
        far[...] = jnp.zeros_like(far)

    for n in range(1, xg.shape[1] // TILE + 1):

        @pl.when(steps == n)
        def _(n=n):
            for i, right in enumerate((xg, xg, pg)):
                for p in range(half):
                    for out, place in ((near, me[0] % 2), (far, 1 - me[0] % 2)):
                        at = pl.multiple_of(i * hid + (2 * p + place) * part, part)
                        out[p, 0, i] = dot(
                            acts[0, : n * TILE, pl.ds(at, part)], right[0, : n * TILE, :], 0, 0
                        ).astype(bf16)


def expert_sum_body(blocks, tokens, offs, so, slots, *refs):
    outs, stage = refs[:blocks], refs[blocks]
    local_count, width = so.shape[0], so.shape[2]
    slot_iota = lax.broadcasted_iota(jnp.int32, (CAP, tokens), 0).astype(f32)
    place = lax.broadcasted_iota(jnp.int32, (CAP, width), 0)
    for b in range(blocks):
        picks = []
        for k in range(local_count):
            off = pl.multiple_of(offs[k, b], 16)
            values = so[k, pl.ds(off, CAP), :]
            stage[b % 2, k * CAP : (k + 1) * CAP, :] = jnp.where(
                place < offs[k, blocks] - off, values.astype(f32), 0.0
            ).astype(bf16)
            picks.append(jnp.where(slot_iota == slots[k, b], 1.0, 0.0).astype(bf16))
        outs[b][...] = dot(jnp.concatenate(picks, 0), stage[b % 2], 0, 0).astype(bf16)


def expert_call(me, base, rows, grads, router, weights):
    hidden_parts, matrices, part, width = weights.shape
    local_count = matrices // 3
    blocks, tokens = len(rows), rows[0].shape[0]
    hid = hidden_parts * part
    most = blocks * CAP
    room = most + TILE

    def weight_spec(m):
        return pl.BlockSpec(
            (hidden_parts, 1, part, width), lambda e: (0, m * local_count + e, 0, 0)
        )

    got = pl.pallas_call(
        functools.partial(expert_body, blocks, tokens),
        grid=(local_count,),
        out_shape=[struct((tokens, width + SIDE))] * blocks
        + [
            struct((local_count, room, 3 * hid)),
            struct((local_count, room, width)),
            struct((local_count, room, width)),
            struct((local_count, room, width)),
            struct((local_count, blocks, 1, tokens), f32),
            struct((local_count, blocks + 1), jnp.int32),
        ],
        in_specs=[SMEM] + [ANY] * (2 * blocks) + [VMEM] + [weight_spec(m) for m in range(3)],
        out_specs=[ANY] * (blocks + 4)
        + [pl.BlockSpec((1, blocks, 1, tokens), lambda e: (e, 0, 0, 0)), SMEM],
        scratch_shapes=[
            pltpu.VMEM((blocks, tokens, width), bf16),
            pltpu.VMEM((blocks, tokens + EXPERTS // 2, width), bf16),
            pltpu.VMEM((blocks, EXPERTS, tokens), f32),
            pltpu.VMEM((blocks, EXPERTS, tokens), f32),
            pltpu.VMEM((room, width), bf16),
            pltpu.VMEM((room, width), bf16),
            pltpu.VMEM((room, width), bf16),
            pltpu.VMEM((room, 3 * hid), bf16),
            pltpu.VMEM((room, 128), f32),
            pltpu.VMEM((local_count, room, width + SIDE), bf16),
            pltpu.VMEM((2, local_count * CAP, width + SIDE), bf16),
            pltpu.VMEM((blocks, tokens, width + SIDE), bf16),
            pltpu.SMEM((local_count, blocks), jnp.int32),
            pltpu.SMEM((1,), jnp.int32),
            pltpu.SemaphoreType.DMA((2 * blocks,)),
            pltpu.SemaphoreType.DMA((4, room // TILE)),
        ],
        compiler_params=pltpu.CompilerParams(vmem_limit_bytes=58 * MIB),
        cost_estimate=pl.CostEstimate(
            flops=10**6, bytes_accessed=10**4, transcendentals=0
        ),
        name="experts",
    )(base, *rows, *grads, router, weights, weights, weights)
    rows_back, (acts, xg, pg, so, slots, offs) = got[:blocks], got[blocks:]

    def grads_of(first, number, acts):
        return pl.pallas_call(
            functools.partial(expert_grad_body, first),
            grid=(number,),
            out_shape=struct((hidden_parts, number, 3, part, width)),
            in_specs=[SMEM]
            + [
                pl.BlockSpec((1, most, n), lambda e: (e + first, 0, 0))
                for n in (3 * hid, width, width)
            ],
            out_specs=pl.BlockSpec((hidden_parts, 1, 3, part, width), lambda e: (0, e, 0, 0, 0)),
            compiler_params=pltpu.CompilerParams(vmem_limit_bytes=60 * MIB),
            cost_estimate=pl.CostEstimate(flops=10**6, bytes_accessed=10**4, transcendentals=0),
            name="expert_grads",
        )(offs, acts, xg, pg)

    def split_grads_of(first, number, acts):
        shape = (hidden_parts // 2, number, 3, part, width)
        out_spec = pl.BlockSpec((hidden_parts // 2, 1, 3, part, width), lambda e: (0, e, 0, 0, 0))
        return pl.pallas_call(
            functools.partial(expert_grad_split_body, first),
            grid=(number,),
            out_shape=(struct(shape), struct(shape)),
            in_specs=[SMEM, SMEM]
            + [
                pl.BlockSpec((1, most, n), lambda e: (e + first, 0, 0))
                for n in (3 * hid, width, width)
            ],
            out_specs=(out_spec, out_spec),
            compiler_params=pltpu.CompilerParams(vmem_limit_bytes=60 * MIB),
            cost_estimate=pl.CostEstimate(flops=10**6, bytes_accessed=10**4, transcendentals=0),
            name="expert_grads",
        )(me, offs, acts, xg, pg)

    def outs_of(so):
        return call(
            functools.partial(expert_sum_body, blocks, tokens),
            [struct((tokens, width))] * blocks,
            (offs, so, slots),
            scratch=[pltpu.VMEM((2, local_count * CAP, width), bf16)],
            smem=1,
            name="expert_sum",
            mib=60,
            flops=10**6,
            nbytes=10**4,
        )

    return rows_back, acts, so, grads_of, split_grads_of, outs_of


def after(values, first):
    return lax.optimization_barrier((values, first))


def flip(values, axis, bit):
    n = lax.axis_size(axis)
    return lax.ppermute(values, axis, [(i, i ^ bit) for i in range(n)])


def gather_hidden(block):
    blocks, marks = [block], [0]
    bit = lax.axis_size("hidden") // 2
    while bit:
        blocks, marks = blocks + [flip(b, "hidden", bit) for b in blocks], marks + [m ^ bit for m in marks]
        bit //= 2
    return blocks, marks


def sum_hidden(keep):
    bit = 1
    n = lax.axis_size("hidden")
    while bit < n:
        far = {m: flip(keep[m], "hidden", bit) for m in keep if m & bit}
        near = {m: keep[m] for m in keep if not m & bit}
        if 2 * bit == n:
            return near[0], far[bit]
        keep = {m: (near[m].astype(f32) + far[m ^ bit].astype(f32)).astype(bf16) for m in near}
        bit *= 2


def shift(values, by):
    n = lax.axis_size("expert")
    return lax.ppermute(values, "expert", [(i, (i + 2 * by) % n) for i in range(n)])


def gather_expert(block, before=()):
    n = lax.axis_size("expert")
    if n != 8:
        whole = lax.all_gather(block, "expert", axis=0, tiled=False)
        return [whole[i] for i in range(n)], before
    side = flip(block, "expert", 1)
    up = shift(block, 1)
    down = shift(block, -1)
    up_after, (side, *before) = after(up, [side, *before])
    far = shift(up_after, 1)
    line = [up, far, down]
    return [block] + line + [side] + [flip(b, "expert", 1) for b in line], before


def take_add(near, got, first):
    n, rest = near.shape[0] // 2, near.shape[1:]
    spec = pl.BlockSpec((1,) + rest, lambda i: (2 * i + first,) + (0,) * len(rest))
    return pl.pallas_call(
        add_body,
        grid=(n,),
        out_shape=struct((n,) + rest),
        in_specs=[spec, spec],
        out_specs=pl.BlockSpec((1,) + rest, lambda i: (i,) + (0,) * len(rest)),
        compiler_params=pltpu.CompilerParams(vmem_limit_bytes=10 * MIB),
        cost_estimate=pl.CostEstimate(flops=10**6, bytes_accessed=10**4, transcendentals=0),
        name="take_add",
    )(near, got)


def all_add(a, b):
    rest = a.shape[1:]
    spec = pl.BlockSpec((1,) + rest, lambda i: (i,) + (0,) * len(rest))
    return pl.pallas_call(
        add_body,
        grid=(a.shape[0],),
        out_shape=struct(a.shape),
        in_specs=[spec, spec],
        out_specs=spec,
        compiler_params=pltpu.CompilerParams(vmem_limit_bytes=60 * MIB),
        cost_estimate=pl.CostEstimate(flops=10**6, bytes_accessed=10**4, transcendentals=0),
        name="all_add",
    )(a, b)


def sum_parts(near, far):
    return sum_parts_end(near, *sum_parts_begin(near, flip(far, "hidden", 1)))


def sum_parts_begin(near, got):
    return got, (take_add(near, got, 1) if got.shape[0] > 1 else None)


def sum_parts_end(near, got, far):
    bit = 2
    left = [near]
    while got.shape[0] > 1:
        if got.shape[0] > 2:
            near = take_add(near, got, 0)
            left = [near]
        else:
            left = [near[0], got[0]]
        got = flip(far, "hidden", bit)
        bit *= 2
        if got.shape[0] > 1:
            far = take_add(near, got, 1)
    return left, got[0]


def add_body(a, b, out):
    out[...] = (a[...].astype(f32) + b[...].astype(f32)).astype(bf16)


def add(a, b):
    return call(add_body, struct(a.shape), (a, b), name="add", mib=6)


def sum_expert(parts):
    n = lax.axis_size("expert")
    if n != 8:
        return [
            lax.psum_scatter(jnp.concatenate(parts, 0), "expert", scatter_dimension=0, tiled=True)
        ]
    line = [None] * 4
    for k in (2, 1, 3, 0):
        line[k] = add(parts[k], flip(parts[4 + k], "expert", 1))
    near = add(line[1], shift(line[2], -1))
    return [line[0], shift(near, -1), shift(line[3], 1)]


def sum_expert_beside(parts, begin, works):
    flip_2 = flip(parts[6], "expert", 1)
    held = begin()
    flip_2, held = after(flip_2, held)
    far = add(parts[2], flip_2)

    far, held = works[0](far, held)
    side, _ = after(parts[5], flip_2)
    flip_1 = flip(side, "expert", 1)
    turn_1 = shift(far, -1)
    (flip_1, turn_1), held = after([flip_1, turn_1], held)
    near = add(add(parts[1], flip_1), turn_1)

    near, held = works[1](near, held)
    side, _ = after(parts[7], [flip_1, turn_1])
    flip_3 = flip(side, "expert", 1)
    result_a = shift(near, -1)
    (flip_3, result_a), held = after([flip_3, result_a], held)
    line_3 = add(parts[3], flip_3)

    line_3, held = works[2](line_3, held)
    side, _ = after(parts[4], [flip_3, result_a])
    flip_0 = flip(side, "expert", 1)
    result_b = shift(line_3, 1)
    (flip_0, result_b), held = after([flip_0, result_b], held)
    return [add(parts[0], flip_0), result_a, result_b], held


def local(
    inputs,
    first_gain,
    query_weight,
    key_weight,
    value_weight,
    out_weight,
    second_gain,
    router_weight,
    gate_weight,
    up_weight,
    down_weight,
    routes,
    segments,
    cotangent,
):
    tokens, width = inputs.shape
    hidden_index = lax.axis_index("hidden")
    expert_index = lax.axis_index("expert")
    groups = lax.axis_size("expert")
    hidden_parts = lax.axis_size("hidden")
    local_count = gate_weight.shape[0]
    gain_one, gain_two = first_gain[None, :], second_gain[None, :]
    router = jnp.pad(router_weight, ((0, 0), (0, SIDE - EXPERTS)))
    spectrum = rope_base ** (-jnp.arange(HEAD_DIM // 2, dtype=f32) * 2.0 / HEAD_DIM)
    me = hidden_index.astype(jnp.int32).reshape(1)

    grad_rows = call(
        route_body,
        struct((tokens + EXPERTS // 2, width)),
        (routes, cotangent),
        name="route",
        flops=10**6,
        nbytes=10**4,
    )
    grads, _ = gather_expert(grad_rows)
    kv, normed, cosine, sine = call(
        project_kv_body,
        (
            struct((tokens, 2 * KV + SIDE)),
            struct((tokens, width)),
            struct((tokens, 128), f32),
            struct((tokens, 128), f32),
        ),
        (
            me * tokens,
            inputs,
            gain_one,
            key_weight,
            value_weight,
            jnp.tile(spectrum, 4)[None, :],
            segments[None, :],
        ),
        smem=1,
        name="project_kv",
        flops=10**6,
        nbytes=10**4,
    )
    q = call(
        project_q_body,
        struct((tokens, width)),
        (normed, query_weight, cosine, sine),
        name="project_q",
        flops=10**6,
        nbytes=10**4,
    )
    kvs, marks = gather_hidden(kv)
    nb = len(kvs)
    weights = jnp.concatenate([gate_weight, up_weight, down_weight], axis=0)
    weights, (kvs[1], grads[1], grads[4]) = after(weights, [kvs[1], grads[1], grads[4]])
    weights_all = lax.all_gather(weights, "hidden", axis=0, tiled=False)
    places = jnp.stack([(hidden_index ^ m) * tokens for m in marks]).astype(jnp.int32)
    hidden, ffn, att, lse, gates = call(
        functools.partial(attend_body, nb),
        (
            struct((tokens, width), f32),
            struct((tokens, width)),
            struct((tokens, width)),
            struct((tokens, 128), f32),
            struct((tokens, SIDE), f32),
        ),
        (places, inputs, q, *kvs, out_weight, gain_two, router, routes),
        scratch=[pltpu.VMEM((nb, tokens, tokens), f32)],
        smem=1,
        name="attend",
        flops=10**6,
        nbytes=10**4,
    )
    if groups == 8:
        first = [1, 2, 3, 4, 5, 7]
        ffn_out, held = after(ffn, [grads[i] for i in first])
        for i, g in zip(first, held):
            grads[i] = g
        rows, (grads[6],) = gather_expert(ffn_out, (grads[6],))
    else:
        rows, _ = gather_expert(ffn)

    first_expert = (expert_index * local_count).astype(jnp.int32)
    rows_back, todo = [], []
    chunk = min(CHUNK, groups)
    router_rows = router_weight.T
    for i in range(0, groups, chunk):
        r, *rest = expert_call(
            me,
            first_expert.reshape(1),
            rows[i : i + chunk],
            grads[i : i + chunk],
            router_rows,
            weights_all,
        )
        rows_back += r
        todo.append(rest)
    half_count = (local_count + 1) // 2

    def weight_grads(first, number, held):
        parts = [grads_of(first, number, a) for (_, _, grads_of, _, _), a in zip(todo, held)]
        return parts[0] if len(parts) == 1 else sum(p.astype(f32) for p in parts).astype(bf16)

    def matrix_sum(part):
        return lax.psum_scatter(part, "hidden", scatter_dimension=0, tiled=False)

    pairs = [[c + 2 * i for i in range(hidden_parts // 2)] for c in range(2)]

    def token_sums(held):
        return [o for (_, _, _, _, outs_of), so in zip(todo, held) for o in outs_of(so)]

    all_acts, all_so = [t[0] for t in todo], [t[1] for t in todo]
    rest_count = local_count - half_count
    if groups == 8 and rest_count:

        def begin():
            return weight_grads(0, half_count, all_acts)

        def work_2(values, held):
            dw_halves.append(matrix_sum(held))
            values, acts = after(values, all_acts)
            return values, todo[0][3](half_count, rest_count, acts[0])

        def work_3(values, held):
            values, so = after(values, all_so)
            return values, (held, token_sums(so))

        dw_halves = []
        row_parts, (dw_rest, outs) = sum_expert_beside(
            rows_back, begin, (work_2, work_3, lambda values, held: (values, held))
        )
        row_parts[0], outs = after(row_parts[0], outs)
    else:
        row_parts = sum_expert(rows_back)
        dw_halves = [matrix_sum(weight_grads(0, local_count, all_acts))]
        outs, dw_rest = token_sums(all_so), None

    hidden_grad, branch, logit_grad, gain_share, out_grad = call(
        functools.partial(hidden_back_body, len(row_parts)),
        (
            struct((tokens, width), f32),
            struct((tokens, width)),
            struct((tokens, SIDE)),
            struct((tokens, width)),
            struct((tokens, width)),
        ),
        (*row_parts, hidden, gates, cotangent, gain_two, router, out_weight),
        name="hidden_back",
    )

    def across(near, far):
        return (near, *sum_parts_begin(near, flip(far, "hidden", 1)))

    def weight_parts(left, right, sides=()):
        n = right.shape[1] + (SIDE if sides else 0)
        rows_each = width // groups // hidden_parts
        shape = (hidden_parts // 2, groups, rows_each, n)
        return call(
            functools.partial(weight_body, groups, hidden_parts, len(sides)),
            (struct(shape), struct(shape)),
            (me, left, right, *[v for pair in sides for v in pair]),
            scratch=[pltpu.VMEM((hidden_parts, groups, rows_each, n), bf16)],
            smem=1,
            name="weight_grad",
        )

    def end_over_mesh(left, got):
        half = sum([v.astype(f32) for v in left], got.astype(f32)).astype(bf16)
        got = lax.all_to_all(half, "expert", split_axis=0, concat_axis=0, tiled=True)
        return jnp.sum(got.astype(f32), axis=0)

    spot = jnp.broadcast_to(
        (jnp.arange(SIDE, dtype=jnp.int32) == EXPERTS).astype(bf16)[None, :], (tokens, SIDE)
    )
    first_parts = weight_parts(att, branch, ((ffn, logit_grad), (gain_share, spot)))
    first_parts = across(*first_parts)
    out_grad, first_parts = after(out_grad, first_parts)
    first_left, first_got = sum_parts_end(*first_parts)
    dq, near, far = call(
        functools.partial(attention_back_body, marks),
        (
            struct((tokens, width)),
            struct((nb // 2, tokens, 2 * KV)),
            struct((nb // 2, tokens, 2 * KV)),
        ),
        (places, out_grad, q, *kvs, lse, cosine, sine),
        scratch=[pltpu.VMEM((nb, tokens, tokens), f32)],
        smem=1,
        name="attention_back",
    )
    if groups == 8:
        moe = [flip(o, "expert", 1) for o in outs[4:]]
        far, (first_got, moe[1], moe[2]) = after(far, [first_got, moe[1], moe[2]])
        moved = shift(add(outs[2], moe[2]), -1)
    kv_near, kv_got, kv_far = across(near, far)
    kb = flip(kv_far, "hidden", 2)
    dq, kv_far = after(dq, kv_far)
    query_near, query_got, query_far = across(*weight_parts(normed, dq))
    kb, query_far = after(kb, query_far)
    query_left, query_got = sum_parts_end(query_near, query_got, query_far)
    if dw_rest is not None:
        near, far = dw_rest
        kv_far, far = after(kv_far, far)
        dw_rest = all_add(near, flip(far, "hidden", 1))
        kb, dw_rest = after(kb, dw_rest)
        dw_rest, dw_halves[0] = after(dw_rest, dw_halves[0])
        dw_halves.append(
            lax.psum_scatter(
                dw_rest, "hidden", scatter_dimension=0, axis_index_groups=pairs, tiled=False
            )
        )
    dw_sum = jnp.concatenate(dw_halves, 0).astype(f32)
    input_grad, dkv, gain_share_one = call(
        finish_body,
        (struct((tokens, width)), struct((tokens, 2 * KV)), struct((tokens, width))),
        (
            kv_near,
            kv_got,
            kb,
            dq,
            query_weight,
            key_weight,
            value_weight,
            hidden_grad,
            inputs,
            gain_one,
            cosine,
            sine,
        ),
        name="finish",
        mib=60,
        flops=10**6,
        nbytes=10**4,
    )
    last_near, last_got, last_far = across(*weight_parts(normed, dkv, ((gain_share_one, spot),)))
    if groups == 8:
        last_far, (moe[0], moe[3], moved) = after(last_far, [moe[0], moe[3], moved])
        near = add(add(outs[1], moe[1]), moved)
        moe = [add(outs[0], moe[0]), shift(near, -1), shift(add(outs[3], moe[3]), 1)]
    else:
        moe = sum_expert(outs)
    first_sums = end_over_mesh(first_left, first_got)
    query_sum = end_over_mesh(query_left, query_got)
    last_left, last_got = sum_parts_end(last_near, last_got, last_far)
    last_got, (first_sums, query_sum) = after(last_got, [first_sums, query_sum])
    half = sum([v.astype(f32) for v in last_left], last_got.astype(f32)).astype(bf16)
    got = lax.all_to_all(half, "expert", split_axis=0, concat_axis=0, tiled=True)
    block_out = (hidden + sum(m.astype(f32) for m in moe)).astype(bf16)
    got, (block_out, dw_out) = after(got, [block_out, [dw_sum[:, i] for i in range(3)]])
    last_sums = jnp.sum(got.astype(f32), axis=0)
    return (
        block_out,
        input_grad,
        last_sums[:, 2 * KV + EXPERTS],
        query_sum,
        last_sums[:, :KV],
        last_sums[:, KV : 2 * KV],
        first_sums[:, :width],
        first_sums[:, width + EXPERTS],
        first_sums[:, width : width + EXPERTS],
        *dw_out,
    )


def solution(mesh):
    tokens = P(("expert", "hidden"), None)
    flat = P(("expert", "hidden"))
    units = P("expert", "hidden", None)
    in_specs = (tokens,) + (P(),) * 7 + (units,) * 3 + (tokens, flat, tokens)
    out_specs = (tokens, tokens, flat) + (tokens,) * 4 + (flat, tokens) + (units,) * 3
    return jax.shard_map(local, mesh=mesh, in_specs=in_specs, out_specs=out_specs, check_vma=False)
```
